512 devices in a mesh: dp: 8 (over y, core), frame: 64 (over z, x).
Axes of the slice: x: 4, y: 4, z: 16, core: 2. Of those that a mesh axis runs over, the one named last changes fastest.
Arguments:
- frame_features: bfloat16 [8, 2048, 8, 1536], P('dp', 'frame'), may hold values from -6 to 6
- frame_owner: int32 [8, 2048, 1], P('dp', 'frame'), may hold values from 0 to 63; in each aligned block of 32 rows (0 to 31, 32 to 63, ..., all dimensions but the last counted through in order) no two rows name the same one
- latents: float32 [64, 1536], replicated, may hold values from -10 to 10
- latent_gain: float32 [1536], replicated, may hold values from 0.25 to 1.75
- media_gain: float32 [1536], replicated, may hold values from 0.25 to 1.75
- query_proj: bfloat16 [1536, 512], P(('dp', 'frame')), may hold values from -0.3 to 0.3
- keyval_proj: bfloat16 [1536, 1024], P(('dp', 'frame')), may hold values from -0.3 to 0.3
- grad_output: bfloat16 [8, 64, 64, 512], P('dp', 'frame'), may hold values from -6 to 6
Outputs:
- attended: bfloat16 [8, 64, 64, 512], P('dp', 'frame')
- latent_grad: float32 [64, 1536], replicated
- latent_gain_grad: float32 [1536], replicated
- media_gain_grad: float32 [1536], replicated
The draws below stay inside these ranges and needn't reach their ends.
Inputs may be any that keep to these rules, and one draw needn't show every extreme that they name: `frame_owner`: of the 32 frames of one device, at most 1 belong to one sample, and in every draw some device sends exactly 1 frames to some sample.
All inputs are finite; a program needn't handle non-finite values.
Results may differ from the reference program's by a relative error of at most 0.012.
The reference program's roundings to bfloat16 on the way count: a program that leaves them out, or rounds other values in their place, can miss the bound.
Values may be sent and summed in bfloat16 or wider, within the bound.
A program may use at most 64 MiB of HBM per device.

```python
import math
import jax
import jax.numpy as jnp
import numpy as np
from jax import lax

D = 1536
HEADS = 8
HEAD_DIM = 64
INNER = 512
LATENTS = 64
FRAME_TOK = 8
FR_DEV = 32
CAP = 1
FRAMES_G = 2048
N_DP = 8
N_FRAME = 64


def draw_latents(key, part):
    key = jax.random.fold_in(key, 11)
    normal_key = jax.random.fold_in(key, 0)
    values = jnp.clip(jax.random.normal(normal_key, (LATENTS, D), jnp.float32), -6.0, 6.0)
    return values.astype(jnp.float32)


def draw_query_proj(key, part):
    key = jax.random.fold_in(key, 12)
    values = jnp.clip(jax.random.normal(key, (D, INNER), jnp.float32), -6.0, 6.0) * D ** (-0.5)
    return values.astype(jnp.bfloat16)


def draw_keyval_proj(key, part):
    key = jax.random.fold_in(key, 13)
    values = jnp.clip(jax.random.normal(key, (D, 2 * INNER), jnp.float32), -6.0, 6.0) * D ** (-0.5)
    return values.astype(jnp.bfloat16)


def level_of(own_key, dims, pieces, least, top_value):
    def one(dim, blocks):
        draws = jax.random.uniform(jax.random.fold_in(jax.random.fold_in(own_key, 6), dim), (blocks,), jnp.float32, least / len(pieces), top_value / len(pieces))
        return jnp.repeat(jnp.exp(draws), dims[dim] // blocks).reshape((-1,) + (1,) * (len(dims) - dim - 1))

    gain = one(*pieces[0])
    for cut in pieces[1:]:
        gain = gain * one(*cut)
    return gain


def routed_block(key, own, number, rows, count, top, reach, lean):
    order = jax.random.permutation(key, count)
    crowded, common = portions_of(count, rows * top, reach, lean, True), portions_of(count, rows * top, reach, lean, False)
    places = jnp.arange(count)

    def named(lengths, turn):
        used = int((lengths > 0).sum())
        fixed = max(1, used // 4)
        passed = fixed + (places - fixed + turn * (used - fixed)) % max(1, count - fixed)
        return jnp.zeros((count,), jnp.int32).at[order[jnp.where(places < fixed, places, passed)]].set(jnp.asarray(lengths, jnp.int32))

    lengths = jnp.where(number % 4 == 0, named(crowded, number // 4), named(common, number - number // 4 - 1))
    mixed = jax.random.permutation(jax.random.fold_in(own, 3), count)
    donor, taker = mixed[0:count // 2 * 2:2], mixed[1:count // 2 * 2:2]
    margin = jnp.minimum(lengths[donor] - 1, reach - lengths[taker]) // 2
    margin = jnp.where((donor == order[0]) | (taker == order[0]) | (lengths[taker] == 0), 0, jnp.maximum(margin, 0))
    passed = jax.random.randint(jax.random.fold_in(own, 4), (count // 2,), 0, 1 << 20) % (margin + 1)
    lengths = lengths.at[donor].add(-passed).at[taker].add(passed)
    members = jnp.searchsorted(jnp.cumsum(lengths), jnp.arange(rows * top), side="right").astype(jnp.int32)
    grid = members.reshape(top, rows).T
    grid = grid[jax.random.permutation(jax.random.fold_in(own, 1), rows)]
    turn = jax.random.randint(jax.random.fold_in(own, 2), (rows, 1), 0, top)
    return jnp.take_along_axis(grid, (jnp.arange(top)[None, :] + turn) % top, axis=1)


def portions_of(number_of, total, bound, slope, full):
    portions = [(1 << 20) // math.isqrt(grade ** slope) + 1 for grade in range(1, number_of + 1)]
    largest = bound if full else min(bound, max(-(-total // number_of), total * portions[0] // sum(portions)))
    least = 1 if total - largest >= number_of - 1 else 0
    holding, surplus = [largest] + [least] * (number_of - 1), total - largest - least * (number_of - 1)
    while surplus > 0:
        candidates = [i for i in range(1, number_of) if holding[i] < largest] or [i for i in range(1, number_of) if holding[i] < bound]
        whole, budget = sum([portions[i] for i in candidates]), surplus
        for i in candidates:
            extra = min(bound - holding[i], max(1, budget * portions[i] // whole), surplus)
            holding[i] = holding[i] + extra
            surplus = surplus - extra
    return np.array(holding)


def normal_values(own_key, extent, deviation, bound, cuts=(), kind=jnp.bfloat16):
    result = jax.random.normal(own_key, extent, jnp.float32) * deviation
    if len(cuts) > 0:
        result = level_of(own_key, extent, cuts, -0.22, 0.18) * result
    return jnp.clip(result, min=-bound, max=bound).astype(kind)


def setup_inputs(seed: int = 0) -> dict:
    keys = jax.random.split(jax.random.key(seed), 9)
    frame_features = normal_values(keys[0], (N_DP, FRAMES_G, FRAME_TOK, D), 1.0, 6.0, ((0, 8), (1, 64)))
    frame_owner_keys = jax.random.split(jax.random.fold_in(keys[1], 1), N_DP * FRAMES_G // FR_DEV)
    frame_owner_turns = jax.random.permutation(jax.random.fold_in(keys[1], 3), N_DP * FRAMES_G // FR_DEV)
    frame_owner = jax.vmap(lambda own, number: routed_block(jax.random.fold_in(keys[1], 2), own, number, FR_DEV, N_FRAME, 1, CAP, 1))(frame_owner_keys, frame_owner_turns).reshape((N_DP, FRAMES_G, 1))
    latents = draw_latents(jax.random.fold_in(keys[8], 71), 0)
    latent_gain = jnp.clip(1.0 + 0.15 * jax.random.normal(keys[3], (D,), jnp.float32), 0.25, 1.75)
    media_gain = jnp.clip(1.0 + 0.15 * jax.random.normal(keys[4], (D,), jnp.float32), 0.25, 1.75)
    query_proj = draw_query_proj(jax.random.fold_in(keys[8], 71), 0)
    keyval_proj = draw_keyval_proj(jax.random.fold_in(keys[8], 71), 0)
    grad_output = normal_values(keys[7], (N_DP, N_FRAME, LATENTS, INNER), 1.0, 6.0, ((0, 8), (1, 64)))
    return {"frame_features": frame_features, "frame_owner": frame_owner, "latents": latents, "latent_gain": latent_gain, "media_gain": media_gain, "query_proj": query_proj, "keyval_proj": keyval_proj, "grad_output": grad_output}


def norm_rows(values):
    center = values - lax.optimization_barrier(jnp.mean(values, -1, keepdims=True))
    inverse = lax.rsqrt(lax.optimization_barrier(jnp.mean(center * center, -1, keepdims=True)) + 1e-05)
    return (center * inverse, inverse)

def attend(query, key_rows, live_keys, gradient, head_count):
    inner_width = query.shape[1]
    head_size = inner_width // head_count
    query_heads = query.astype(jnp.float32).reshape(-1, head_count, head_size)
    key_heads = key_rows[:, :inner_width].astype(jnp.float32).reshape(-1, head_count, head_size)
    value_heads = key_rows[:, inner_width:].astype(jnp.float32).reshape(-1, head_count, head_size)
    scores = jnp.einsum('qhd,khd->hqk', query_heads, key_heads)
    scores = jnp.where(live_keys[None, None, :], scores, -jnp.inf)
    weights = jax.nn.softmax(scores, axis=-1)
    weights_low = lax.optimization_barrier(weights.astype(jnp.bfloat16)).astype(jnp.float32)
    attended = jnp.einsum('hqk,khd->qhd', weights_low, value_heads).reshape(-1, inner_width).astype(jnp.bfloat16)
    grad_heads = gradient.astype(jnp.float32).reshape(-1, head_count, head_size)
    grad_weights = jnp.einsum('qhd,khd->hqk', grad_heads, value_heads)
    grad_scores = weights * (grad_weights - lax.optimization_barrier(jnp.sum(weights * grad_weights, -1, keepdims=True)))
    grad_scores = lax.optimization_barrier(grad_scores.astype(jnp.bfloat16)).astype(jnp.float32)
    grad_query = jnp.einsum('hqk,khd->qhd', grad_scores, key_heads).reshape(-1, inner_width)
    grad_key = jnp.einsum('hqk,qhd->khd', grad_scores, query_heads).reshape(-1, inner_width)
    grad_value = jnp.einsum('hqk,qhd->khd', weights_low, grad_heads).reshape(-1, inner_width)
    return (attended, grad_query, jnp.concatenate([grad_key, grad_value], axis=1))

def reference(frame_features, frame_owner, latents, latent_gain, media_gain, query_proj, keyval_proj, grad_output):
    score_scale = HEAD_DIM ** (-0.5)
    latent_hat, latent_inv = norm_rows(latents)
    latent_norm = (latent_hat * latent_gain).astype(jnp.bfloat16)
    query = (jnp.dot(latent_norm, query_proj, preferred_element_type=jnp.float32) * score_scale).astype(jnp.bfloat16)
    latent_keyval = jnp.dot(latent_norm, keyval_proj, preferred_element_type=jnp.float32).astype(jnp.bfloat16)
    most_frames = N_FRAME * CAP
    media_len = most_frames * FRAME_TOK

    def group(inputs):
        frames, route, gradient = inputs
        media_hat, _ = norm_rows(frames.astype(jnp.float32))
        media_norm = (media_hat * media_gain).astype(jnp.bfloat16)
        media_keyval = jnp.dot(media_norm.reshape(-1, D), keyval_proj, preferred_element_type=jnp.float32)
        media_keyval = media_keyval.astype(jnp.bfloat16).reshape(FRAMES_G, FRAME_TOK, 2 * INNER)
        sorted_frames = jnp.argsort(route, stable=True).astype(jnp.int32)
        counts = lax.optimization_barrier(jnp.sum((route[None, :] == jnp.arange(N_FRAME, dtype=jnp.int32)[:, None]).astype(jnp.int32), axis=1))
        starts = (jnp.cumsum(counts) - counts).astype(jnp.int32)
        padded = jnp.concatenate([sorted_frames, jnp.zeros((most_frames,), jnp.int32)])

        def owner(owner_inputs):
            position, owner_grad = owner_inputs
            chosen = lax.dynamic_slice_in_dim(padded, starts[position], most_frames).astype(jnp.int32)
            live_frames = jnp.arange(most_frames, dtype=jnp.int32) < counts[position]
            key_rows = jnp.concatenate([media_keyval[chosen].reshape(-1, 2 * INNER), latent_keyval], axis=0)
            live_keys = jnp.concatenate([jnp.repeat(live_frames, FRAME_TOK), jnp.ones((LATENTS,), bool)])
            attended, grad_query, grad_keyval = attend(query, key_rows, live_keys, owner_grad, HEADS)
            grad_media = grad_keyval[:media_len].reshape(most_frames, FRAME_TOK, 2 * INNER)
            grad_media = jnp.where(live_frames[:, None, None], grad_media, 0.0).astype(jnp.bfloat16)
            return (attended, grad_query * score_scale, grad_keyval[media_len:], chosen, grad_media)
        attended, grad_query, grad_latent_kv, chosen, grad_media = lax.map(owner, (jnp.arange(N_FRAME, dtype=jnp.int32), gradient))
        per_frame = jnp.zeros((FRAMES_G, FRAME_TOK, 2 * INNER), jnp.float32)
        per_frame = per_frame.at[chosen.reshape(-1)].add(grad_media.astype(jnp.float32).reshape(-1, FRAME_TOK, 2 * INNER))
        grad_norm = lax.dot_general(per_frame.astype(jnp.bfloat16).reshape(-1, 2 * INNER), keyval_proj, (((1,), (1,)), ((), ())), preferred_element_type=jnp.float32).astype(jnp.bfloat16)
        media_term = lax.optimization_barrier(jnp.sum(grad_norm.astype(jnp.float32).reshape(FRAMES_G, FRAME_TOK, D) * media_hat, axis=(0, 1)))
        return (attended, lax.optimization_barrier(jnp.sum(grad_query, axis=0)), lax.optimization_barrier(jnp.sum(grad_latent_kv, axis=0)), media_term)
    attended, query_sums, latent_sums, media_terms = lax.map(group, (frame_features, frame_owner[:, :, 0], grad_output))
    query_sum = lax.optimization_barrier(jnp.sum(query_sums, axis=0))
    latent_sum = lax.optimization_barrier(jnp.sum(latent_sums, axis=0))
    media_gain_grad = lax.optimization_barrier(jnp.sum(media_terms, axis=0))
    from_query = lax.dot_general(query_sum, query_proj.astype(jnp.float32), (((1,), (1,)), ((), ())), precision=lax.Precision.HIGHEST)
    from_keyval = lax.dot_general(latent_sum, keyval_proj.astype(jnp.float32), (((1,), (1,)), ((), ())), precision=lax.Precision.HIGHEST)
    grad_latent_norm = from_query + from_keyval
    latent_gain_grad = lax.optimization_barrier(jnp.sum(grad_latent_norm * latent_hat, axis=0))
    grad_hat = grad_latent_norm * latent_gain
    latent_grad = latent_inv * (grad_hat - lax.optimization_barrier(jnp.mean(grad_hat, -1, keepdims=True)) - latent_hat * lax.optimization_barrier(jnp.mean(grad_hat * latent_hat, -1, keepdims=True)))
    return (attended, latent_grad, latent_gain_grad, media_gain_grad)
```

```python
import jax
import jax.numpy as jnp
from jax import lax
from jax.experimental import pallas as pl
from jax.experimental.pallas import tpu as pltpu
from jax.sharding import PartitionSpec as P

NX, NY, NZ = 4, 4, 16
NP = NX * NY
MESH = pl.DeviceIdType.MESH
VM = pl.BlockSpec(memory_space=pltpu.VMEM)


def place():
    dp = lax.axis_index("dp")
    fr = lax.axis_index("frame")
    return lax.div(dp, 2), lax.rem(dp, 2), lax.div(fr, NX), lax.rem(fr, NX)


def device(y, core, z, x):
    return (y * 2 + core, z * NX + x)


def push(src, dst, send, recv, to):
    return pltpu.make_async_remote_copy(
        src_ref=src, dst_ref=dst, send_sem=send, recv_sem=recv, device_id=to, device_id_type=MESH
    )


def greet(barrier, to):
    pl.semaphore_signal(barrier, inc=1, device_id=to, device_id_type=MESH)


def gather_kernel(w_ref, full, pair, pair_rows, zbuf, rows, send0, recv0, send1, recv1, send2, recv2, send3, recv3, send4, recv4):
    y, core, z, x = place()
    other = 1 - core
    partner = device(y, other, z, x)

    barrier = pltpu.get_barrier_semaphore()
    greet(barrier, partner)

    @pl.loop(1, NZ)
    def _(k):
        greet(barrier, device(y, core, lax.rem(z + k, NZ), x))

    @pl.loop(1, NX)
    def _(k):
        greet(barrier, device(y, core, z, lax.rem(x + k, NX)))

    @pl.loop(1, NY)
    def _(k):
        greet(barrier, device(lax.rem(y + k, NY), core, z, x))

    pl.semaphore_wait(barrier, 1 + NZ - 1 + NX - 1 + NY - 1)

    swap = push(w_ref.at[other], pair.at[core], send0, recv0, partner)
    swap.start()
    pair[core] = w_ref[core]
    swap.wait()
    pair_rows[...] = jnp.zeros_like(pair_rows)
    pair_rows[0:3] = pair[0, 0:3].astype(jnp.float32)
    pair_rows[3:6] = pair[1, 0:3].astype(jnp.float32)
    zbuf[z] = pair_rows[...].astype(jnp.bfloat16)

    def along_z(k):
        return push(zbuf.at[z], zbuf.at[z], send1.at[k], recv1.at[k], device(y, core, lax.rem(z + k, NZ), x))

    @pl.loop(1, NZ)
    def _(k):
        along_z(k).start()

    @pl.loop(1, NZ)
    def _(k):
        along_z(k).wait_recv()

    for k in range(NZ):
        rows[6 * k:6 * k + 6] = zbuf[k, 0:6].astype(jnp.float32)
    full[core, y, x] = rows[...].astype(jnp.bfloat16)

    def second(k):
        to = device(lax.rem(y + k * other, NY), core, z, lax.rem(x + k * core, NX))
        block = full.at[core, y, x]
        return push(block, block, send2.at[k], recv2.at[k], to)

    def third(k, yy, xx, turn):
        to = device(lax.rem(y + k * core, NY), core, z, lax.rem(x + k * other, NX))
        block = full.at[core, yy, xx]
        return push(block, block, send3.at[turn, k], recv3.at[turn, k], to)

    def fourth(yy, xx):
        block = full.at[core, yy, xx]
        return push(block, block, send4.at[yy, xx], recv4.at[yy, xx], partner)

    def late(k):
        return lax.rem(y + (4 - k) * other, NY), lax.rem(x + (4 - k) * core, NX)

    @pl.loop(1, 4)
    def _(k):
        second(k).start()

    @pl.loop(1, 4)
    def _(k):
        third(k, y, x, 0).start()

    fourth(y, x).start()

    @pl.loop(1, 4)
    def _(turn):
        second(turn).wait_recv()
        yy, xx = late(turn)

        @pl.loop(1, 4)
        def _(k):
            third(k, yy, xx, turn).start()

        fourth(yy, xx).start()

    @pl.loop(0, 4)
    def _(turn):
        yy, xx = late(turn)

        @pl.loop(1, 4)
        def _(k):
            third(k, yy, xx, turn).wait_recv()
            fourth(lax.rem(yy + (4 - k) * core, NY), lax.rem(xx + (4 - k) * other, NX)).start()

    @pl.loop(0, NP)
    def _(i):
        fourth(lax.div(i, NX), lax.rem(i, NX)).wait()

    @pl.loop(1, NZ)
    def _(k):
        along_z(k).wait_send()

    @pl.loop(1, 4)
    def _(k):
        second(k).wait_send()

    @pl.loop(0, 4)
    def _(turn):
        yy, xx = late(turn)

        @pl.loop(1, 4)
        def _(k):
            third(k, yy, xx, turn).wait_send()


def gather_weights(shard):
    dma = pltpu.SemaphoreType.DMA
    return pl.pallas_call(
        gather_kernel,
        out_shape=jax.ShapeDtypeStruct((2, NY, NX, 6 * NZ, 768), jnp.bfloat16),
        in_specs=[VM],
        out_specs=VM,
        scratch_shapes=[
            pltpu.VMEM((2, 8, 768), jnp.bfloat16),
            pltpu.VMEM((8, 768), jnp.float32),
            pltpu.VMEM((NZ, 8, 768), jnp.bfloat16),
            pltpu.VMEM((6 * NZ, 768), jnp.float32),
            dma, dma, dma((NZ,)), dma((NZ,)), dma((4,)), dma((4,)),
            dma((4, 4)), dma((4, 4)), dma((NY, NX)), dma((NY, NX)),
        ],
        compiler_params=pltpu.CompilerParams(collective_id=0, has_side_effects=True, vmem_limit_bytes=40 << 20),
        name="gather_weights",
    )(shard)


def total_kernel(x_ref, out, r0, r1, r2, acc, done, send0, recv0, send1, recv1, send2, recv2, send3, recv3, send4, recv4, send5, recv5):
    y, core, z, x = place()
    me = y * NX + x
    other = 1 - core
    partner = device(y, other, z, x)

    def plane(k):
        p = lax.rem(me + k, NP)
        return p, device(lax.div(p, NX), core, z, lax.rem(p, NX))

    def column(k):
        zz = lax.rem(z + k, NZ)
        return zz, device(y, core, zz, x)

    barrier = pltpu.get_barrier_semaphore()
    greet(barrier, partner)

    @pl.loop(1, NP)
    def _(k):
        greet(barrier, plane(k)[1])

    @pl.loop(1, NZ)
    def _(k):
        greet(barrier, column(k)[1])

    pl.semaphore_wait(barrier, 1 + NP - 1 + NZ - 1)

    swap = push(x_ref.at[other], r0, send0, recv0, partner)
    swap.start()
    swap.wait()

    @pl.loop(0, NP)
    def _(p):
        acc[p] = x_ref[core, p] + r0[p]

    def first(k):
        p, to = plane(k)
        return push(acc.at[p], r1.at[me], send1.at[k], recv1.at[k], to)

    @pl.loop(1, NP)
    def _(k):
        first(k).start()

    r1[me] = acc[me]

    @pl.loop(1, NP)
    def _(k):
        first(k).wait()

    part = r1[0]
    for p in range(1, NP):
        part = part + r1[p]
    acc[me] = part

    def second(k):
        zz, to = column(k)
        return push(acc.at[me, zz], r2.at[z], send2.at[k], recv2.at[k], to)

    @pl.loop(1, NZ)
    def _(k):
        second(k).start()

    r2[z] = acc[me, z]

    @pl.loop(1, NZ)
    def _(k):
        second(k).wait()

    whole = r2[0]
    for p in range(1, NZ):
        whole = whole + r2[p]
    done[...] = whole
    out[core, me, z] = whole

    def third(k):
        return push(done, out.at[core, me, z], send3.at[k], recv3.at[k], column(k)[1])

    @pl.loop(1, NZ)
    def _(k):
        third(k).start()

    @pl.loop(1, NZ)
    def _(k):
        third(k).wait()

    def fourth(k):
        return push(out.at[core, me], out.at[core, me], send4.at[k], recv4.at[k], plane(k)[1])

    @pl.loop(1, NP)
    def _(k):
        fourth(k).start()

    def fifth(p):
        return push(out.at[core, p], out.at[core, p], send5.at[p], recv5.at[p], partner)

    fifth(me).start()

    @pl.loop(1, NP)
    def _(k):
        fourth(k).wait()
        fifth(lax.rem(me + NP - k, NP)).start()

    @pl.loop(0, NP)
    def _(p):
        fifth(p).wait()


def total(parts):
    dma = pltpu.SemaphoreType.DMA
    f32 = jnp.float32
    return pl.pallas_call(
        total_kernel,
        out_shape=jax.ShapeDtypeStruct((2, NP, NZ, 2, 128), f32),
        in_specs=[VM],
        out_specs=VM,
        scratch_shapes=[
            pltpu.VMEM((NP, NZ, 2, 128), f32),
            pltpu.VMEM((NP, NZ, 2, 128), f32),
            pltpu.VMEM((NZ, 2, 128), f32),
            pltpu.VMEM((NP, NZ, 2, 128), f32),
            pltpu.VMEM((2, 128), f32),
            dma, dma, dma((NP,)), dma((NP,)), dma((NZ,)), dma((NZ,)),
            dma((NZ,)), dma((NZ,)), dma((NP,)), dma((NP,)), dma((NP,)), dma((NP,)),
        ],
        compiler_params=pltpu.CompilerParams(collective_id=1, has_side_effects=True, vmem_limit_bytes=40 << 20),
        name="total",
    )(parts)

HEADS = 8


def norm_rows(values):
    center = values - jnp.mean(values, -1, keepdims=True)
    inverse = lax.rsqrt(jnp.mean(center * center, -1, keepdims=True) + 1e-05)
    return (center * inverse, inverse)


def attend(query, key_rows, live_keys, gradient, head_count):
    inner_width = query.shape[1]
    head_size = inner_width // head_count
    query_heads = query.reshape(-1, head_count, head_size)
    key_heads = key_rows[:, :inner_width].reshape(-1, head_count, head_size)
    value_heads = key_rows[:, inner_width:].reshape(-1, head_count, head_size)
    scores = jnp.einsum("qhd,khd->hqk", query_heads, key_heads, preferred_element_type=jnp.float32)
    scores = jnp.where(live_keys[None, None, :], scores, -jnp.inf)
    weights = jax.nn.softmax(scores, axis=-1)
    weights_low = weights.astype(jnp.bfloat16)
    attended = jnp.einsum(
        "hqk,khd->qhd", weights_low, value_heads, preferred_element_type=jnp.float32
    )
    attended = attended.reshape(-1, inner_width).astype(jnp.bfloat16)
    grad_heads = gradient.reshape(-1, head_count, head_size)
    grad_weights = jnp.einsum(
        "qhd,khd->hqk", grad_heads, value_heads, preferred_element_type=jnp.float32
    )
    grad_scores = weights * (grad_weights - jnp.sum(weights * grad_weights, -1, keepdims=True))
    grad_scores = grad_scores.astype(jnp.bfloat16)
    grad_query = jnp.einsum(
        "hqk,khd->qhd", grad_scores, key_heads, preferred_element_type=jnp.float32
    )
    grad_key = jnp.einsum(
        "hqk,qhd->khd", grad_scores, query_heads, preferred_element_type=jnp.float32
    )
    grad_value = jnp.einsum(
        "hqk,qhd->khd", weights_low, grad_heads, preferred_element_type=jnp.float32
    )
    grad_keyval = jnp.concatenate(
        [grad_key.reshape(-1, inner_width), grad_value.reshape(-1, inner_width)], axis=1
    )
    return (attended, grad_query.reshape(-1, inner_width), grad_keyval)


def natural_order():
    place = jnp.arange(384)
    gathered = place // 96, place % 96 // 6, place % 6 // 3, place % 3
    natural = gathered[2] * 192 + gathered[1] * 12 + gathered[0] * 3 + gathered[3]
    return (jnp.arange(384)[:, None] == natural[None, :]).astype(jnp.bfloat16)


def reorder(rows, order, side):
    dims = (((1,), (side,)), ((), ()))
    blocks = rows.reshape(-1, 384)
    return lax.dot_general(blocks, order, dims, preferred_element_type=jnp.float32).astype(rows.dtype).reshape(rows.shape)


def reorder_precise(rows, order):
    blocks = rows.reshape(-1, 384)
    result = 0.0
    for _ in range(3):
        part = blocks.astype(jnp.bfloat16)
        blocks = blocks - part.astype(jnp.float32)
        result = result + lax.dot_general(part, order, (((1,), (1,)), ((), ())), preferred_element_type=jnp.float32)
    return result.reshape(rows.shape)


def both(left, right, first, second, side):
    dims = (((1,), (side,)), ((), ()))
    return (
        lax.dot_general(left, first, dims, preferred_element_type=jnp.float32),
        lax.dot_general(right, second, dims, preferred_element_type=jnp.float32),
    )


def precise_both(left, right, first, second):
    result = 0.0
    for _ in range(2):
        high = left.astype(jnp.bfloat16), right.astype(jnp.bfloat16)
        one, two = both(*high, first, second, 1)
        result = result + one + two
        left, right = left - high[0].astype(jnp.float32), right - high[1].astype(jnp.float32)
    return result


def body(
    frame_features,
    frame_owner,
    latents,
    latent_gain,
    media_gain,
    query_proj,
    keyval_proj,
    grad_output,
):
    owners = lax.axis_size("frame")
    inner = query_proj.shape[1]
    score_scale = (inner // HEADS) ** (-0.5)
    half = inner // 2
    shard = jnp.stack(
        [
            jnp.concatenate([keyval_proj[:, :inner], query_proj[:, :half]], axis=1),
            jnp.concatenate([keyval_proj[:, inner:], query_proj[:, half:]], axis=1),
        ]
    )
    full = gather_weights(jnp.pad(shard, ((0, 0), (0, 5), (0, 0)))).reshape(2, 1536, 768)
    key_proj, value_proj = full[0, :, :inner], full[1, :, :inner]
    query_left, query_right = full[0, :, inner:], full[1, :, inner:]
    order = natural_order()

    def project(rows, first, second):
        return jnp.concatenate(both(rows, rows, first, second, 0), axis=1)

    latent_hat, latent_inv = norm_rows(latents)
    latent_norm = reorder((latent_hat * latent_gain).astype(jnp.bfloat16), order, 0)
    query = (project(latent_norm, query_left, query_right) * score_scale).astype(jnp.bfloat16)
    latent_keyval = project(latent_norm, key_proj, value_proj).astype(jnp.bfloat16)
    frames = frame_features[0]
    frame_count, frame_tokens, width = frames.shape
    media_hat, _ = norm_rows(frames.astype(jnp.float32).reshape(-1, width))
    media_norm = reorder((media_hat * media_gain).astype(jnp.bfloat16), order, 0)
    media_keyval = project(media_norm, key_proj, value_proj).astype(jnp.bfloat16)
    route = frame_owner[0, :, 0]
    selected = route[None, :] == jnp.arange(owners, dtype=jnp.int32)[:, None]
    slot_live = jnp.sum(selected.astype(jnp.int32), axis=1).reshape(owners, 1)
    selector = selected.astype(jnp.bfloat16)
    packed = jnp.dot(selector, media_keyval.reshape(frame_count, -1), preferred_element_type=jnp.float32)
    received = lax.all_to_all(
        packed.astype(jnp.bfloat16).reshape(owners, frame_tokens, -1), "frame", split_axis=0, concat_axis=0, tiled=True
    )
    live_slots = lax.all_to_all(slot_live, "frame", split_axis=0, concat_axis=0, tiled=True)
    media_rows = owners * frame_tokens
    key_rows = jnp.concatenate([received.reshape(media_rows, -1), latent_keyval], axis=0)
    live_keys = jnp.concatenate(
        [jnp.repeat(live_slots.reshape(-1) > 0, frame_tokens), jnp.ones((latents.shape[0],), bool)]
    )
    attended, grad_query, grad_keyval = attend(query, key_rows, live_keys, grad_output[0, 0], HEADS)
    grad_media = grad_keyval[:media_rows].astype(jnp.bfloat16).reshape(owners, frame_tokens, -1)
    returned = lax.all_to_all(grad_media, "frame", split_axis=0, concat_axis=0, tiled=True)
    frame_rows = lax.dot_general(
        selector, returned.reshape(owners, -1), (((0,), (0,)), ((), ())), preferred_element_type=jnp.float32
    )
    frame_grad = frame_rows.astype(jnp.bfloat16).reshape(frame_count * frame_tokens, -1)
    from_key, from_value = both(frame_grad[:, :inner], frame_grad[:, inner:], key_proj, value_proj, 1)
    grad_norm = reorder((from_key + from_value).astype(jnp.bfloat16), order, 1)
    media_term = jnp.sum(grad_norm.astype(jnp.float32) * media_hat, axis=0)
    sums = jnp.concatenate([grad_query * score_scale, grad_keyval[media_rows:]], axis=1)
    flat = jnp.concatenate([sums.reshape(-1), media_term, jnp.zeros((131072 - sums.size - width,), jnp.float32)])
    flat = total(flat.reshape(2, NP, NZ, 2, 128)).reshape(-1)
    sums, media_gain_grad = flat[: sums.size].reshape(sums.shape), flat[sums.size : sums.size + width]
    grad_latent_norm = precise_both(sums[:, :half], sums[:, half:inner], query_left, query_right)
    grad_latent_norm = grad_latent_norm + precise_both(
        sums[:, inner : 2 * inner], sums[:, 2 * inner :], key_proj, value_proj
    )
    grad_latent_norm = reorder_precise(grad_latent_norm, order)
    latent_gain_grad = jnp.sum(grad_latent_norm * latent_hat, axis=0)
    grad_hat = grad_latent_norm * latent_gain
    latent_grad = latent_inv * (
        grad_hat
        - jnp.mean(grad_hat, -1, keepdims=True)
        - latent_hat * jnp.mean(grad_hat * latent_hat, -1, keepdims=True)
    )
    return (attended[None, None], latent_grad, latent_gain_grad, media_gain_grad)


def solution(mesh):
    placed = (
        P("dp", "frame", None, None),
        P("dp", "frame", None),
        P(),
        P(),
        P(),
        P(("dp", "frame"), None),
        P(("dp", "frame"), None),
        P("dp", "frame", None, None),
    )
    return jax.shard_map(
        body,
        mesh=mesh,
        in_specs=placed,
        out_specs=(P("dp", "frame", None, None), P(), P(), P()),
        check_vma=False,
    )
```

```python
import jax
import jax.numpy as jnp
import numpy as np
from jax import lax
from jax.experimental import pallas as pl
from jax.experimental.pallas import tpu as pltpu
from jax.sharding import PartitionSpec as P

NX, NY, NZ = 4, 4, 16
NP = NX * NY
HEADS, HEAD, INNER, WIDTH, LAT = 8, 64, 512, 1536, 64
TOK, FRAMES = 8, 32
ROWS = FRAMES * TOK
KEYS = NX * TOK
SLOTS = NZ * TOK
SEND = 2 * INNER + 128
DEAD = -1e30
MESH = pl.DeviceIdType.MESH
F32, BF16 = jnp.float32, jnp.bfloat16
DMA = pltpu.SemaphoreType.DMA


def gathered_order():
    place = np.arange(384)
    natural = place % 6 // 3 * 192 + place % 96 // 6 * 12 + place // 96 * 3 + place % 3
    return (np.arange(384)[:, None] == natural[None, :]).astype(np.float32)


def sample_order():
    place = np.arange(NZ * KEYS)
    source = place % KEYS // TOK * SLOTS + place // KEYS * TOK + place % TOK
    return (source[:, None] == np.arange(NZ * KEYS)[None, :]).astype(np.float32)


def dot(left, right, dims=((1,), (0,))):
    return lax.dot_general(left, right, (dims, ((), ())), preferred_element_type=F32)


def dot_nt(left, right):
    return dot(left, right, ((1,), (1,)))


def dot_tn(left, right):
    return dot(left, right, ((0,), (0,)))


def norm_rows(values):
    center = values - jnp.mean(values, -1, keepdims=True)
    inverse = lax.rsqrt(jnp.mean(center * center, -1, keepdims=True) + 1e-05)
    return center * inverse, inverse


def iota(shape, dim):
    return lax.broadcasted_iota(jnp.int32, shape, dim)


def by_head(rows):
    shape = (HEADS * LAT, INNER)
    same = (iota(shape, 0) >> 6) == (iota(shape, 1) >> 6)
    return jnp.where(same, jnp.concatenate([rows.astype(F32)] * HEADS, axis=0), 0.0).astype(BF16)


def head_blocks(left, right):
    blocks = []
    for pair in range(HEADS // 2):
        lanes = slice(pair * 128, pair * 128 + 128)
        both = dot_tn(left[:, lanes], right[:, lanes])
        blocks.append(jnp.where(iota((HEAD, 128), 1) < HEAD, both[:HEAD], both[HEAD:]))
    return jnp.concatenate(blocks, axis=1)


def push(src, dst, send, recv, to):
    return pltpu.make_async_remote_copy(
        src_ref=src, dst_ref=dst, send_sem=send, recv_sem=recv, device_id=to, device_id_type=MESH
    )


INPUTS = ("shard", "frames", "latents", "latent_gain", "media_gain", "route_lane", "route_rows", "grad", "order", "sorting")
OUTPUTS = ("attended", "latent_grad", "latent_gain_grad", "media_gain_grad")
BUFFERS = dict(
    pair=((2, 8, 768), BF16),
    pair_rows=((8, 768), F32),
    zbuf=((NZ, 8, 768), BF16),
    rows=((6 * NZ, 768), F32),
    wkv=((2, 2, NY, NX, 6 * NZ, 256), BF16),
    wq=((2, 2, NY, NX, 6 * NZ, 128), BF16),
    gob=((NZ, LAT, INNER), BF16),
    hat=((ROWS, WIDTH), F32),
    normed=((ROWS, WIDTH), BF16),
    kv=((ROWS, 2 * INNER), BF16),
    slots=((NX, SLOTS, SEND), BF16),
    got=((NX, SLOTS, SEND), BF16),
    kvs=((NZ, KEYS, SEND), BF16),
    lat_normed=((LAT, WIDTH), BF16),
    lat_kv=((LAT, 2 * INNER), BF16),
    qrow=((HEADS * LAT, INNER), BF16),
    gorow=((NZ, HEADS * LAT, INNER), BF16),
    scores=((NZ, KEYS, INNER), F32),
    gprob=((NZ, KEYS, INNER), F32),
    lat_scores=((LAT, INNER), F32),
    lat_gprob=((LAT, INNER), F32),
    stat=((NZ, 3, 1, INNER), F32),
    stat_got=((NZ, 3, 1, INNER), F32),
    stat_own=((3, 1, INNER), F32),
    stat_all=((NZ, 3, 1, INNER), F32),
    gs=((NZ, KEYS, INNER), BF16),
    gkv=((NZ, KEYS, 2 * INNER), BF16),
    back=((NX, SLOTS, 2 * INNER), BF16),
    back_got=((NX, SLOTS, 2 * INNER), BF16),
    part=((NZ, LAT, INNER), F32),
    lat_out=((4, LAT, INNER), F32),
    ring_out=((2, 9, LAT, INNER), BF16),
    ring_in=((2, 9, LAT, INNER), BF16),
    sums=((2, NP, 3, 8, 128), F32),
    sums_core=((NP, 3, 8, 128), F32),
    sums_plane=((NP, 3, 8, 128), F32),
    media=((NP, 1, 128), F32),
    media_core=((NP, 1, 128), F32),
    media_plane=((NP, 1, 128), F32),
    chunk=((4, 8, 128), F32),
    chunk_got=((4, NZ, 8, 128), F32),
    whole=((2, NP, 4, 8, 128), F32),
)
SEMS = dict(
    swap=(1,), along_z=(NZ,), go=(2, 9), kv2=(2, 4), kv3=(2, 4), kv4=(2, 4), q2=(2, 4), q3=(2, 4), q4=(2, 4),
    out_x=(4,), back_x=(4,), stat_to=(NZ,), stat_from=(NZ,), ring=(2, 9),
    sum_core=(1,), sum_plane=(NP,), med_core=(1,), med_plane=(NP,), red_z=(4, NZ), all_z=(4, NZ), all_plane=(NP,), all_core=(NP,),
)


class Refs:
    pass


def kernel(*refs):
    r = Refs()
    names = INPUTS + OUTPUTS + tuple(BUFFERS) + tuple(n + e for n in SEMS for e in ("_s", "_r"))
    for name, ref in zip(names, refs, strict=True):
        setattr(r, name, ref)

    def sems(name, *at):
        return getattr(r, name + "_s").at[at], getattr(r, name + "_r").at[at]

    dp, fr = lax.axis_index("dp"), lax.axis_index("frame")
    y, core, z, x = lax.div(dp, 2), lax.rem(dp, 2), lax.div(fr, NX), lax.rem(fr, NX)
    other, me = 1 - core, y * NX + x

    def device(yy, cc, zz, xx):
        return (yy * 2 + cc, zz * NX + xx)

    partner = device(y, other, z, x)

    def at_z(k):
        zz = lax.rem(z + k, NZ)
        return zz, device(y, core, zz, x)

    def at_x(k):
        xx = lax.rem(x + k, NX)
        return xx, device(y, core, z, xx)

    def at_y(k):
        yy = lax.rem(y + k, NY)
        return yy, device(yy, core, z, x)

    def at_plane(k):
        p = lax.rem(me + k, NP)
        return p, device(lax.div(p, NX), core, z, lax.rem(p, NX))

    def each(lo, hi, act):
        @pl.loop(lo, hi)
        def _(k):
            act(k)

    barrier = pltpu.get_barrier_semaphore()

    def greet(to):
        pl.semaphore_signal(barrier, inc=1, device_id=to, device_id_type=MESH)

    each(1, NZ, lambda k: greet(at_z(k)[1]))
    each(1, NP, lambda k: greet(at_plane(k)[1]))
    greet(partner)
    r.pair[core] = r.shard[core]
    r.gob[z] = r.grad[...]

    def norm_frames(i):
        @pl.loop(i * 2, i * 2 + 2)
        def _(b):
            span = pl.ds(pl.multiple_of(b * 32, 32), 32)
            hat, _ = norm_rows(r.frames[span, :].astype(F32))
            r.hat[span, :] = hat
            r.normed[span, :] = (hat * r.media_gain[...]).astype(BF16)

    def reorder(ref):
        for i in range(4):
            lanes = slice(i * 384, i * 384 + 384)
            ref[:, lanes] = dot(ref[:, lanes], r.order[...]).astype(BF16)

    pl.semaphore_wait(barrier, NZ - 1 + NP - 1 + 1)

    swap = push(r.shard.at[other], r.pair.at[core], *sems("swap", 0), partner)
    swap.start()

    def go(way, s):
        slot = lax.rem(z + (NZ + 1 - s if way == 0 else s - 1), NZ)
        to = at_z(1 if way == 0 else NZ - 1)[1]
        return push(r.gob.at[slot], r.gob.at[slot], *sems("go", way, s), to)

    def go_start(s):
        go(0, s).start()
        if s < 8:
            go(1, s).start()

    def go_next(s):
        go(0, s).wait_recv()
        if s < 8:
            go(1, s).wait_recv()
            go_start(s + 1)

    swap.wait()
    r.pair_rows[...] = jnp.zeros_like(r.pair_rows)
    r.pair_rows[0:3] = r.pair[0, 0:3].astype(F32)
    r.pair_rows[3:6] = r.pair[1, 0:3].astype(F32)
    r.zbuf[z] = r.pair_rows[...].astype(BF16)

    def along_z(k):
        return push(r.zbuf.at[z], r.zbuf.at[z], *sems("along_z", k), at_z(k)[1])

    each(1, NZ, lambda k: along_z(k).start())
    go_start(1)
    norm_frames(0)
    norm_frames(1)
    go_next(1)
    each(1, NZ, lambda k: along_z(k).wait_recv())
    for k in range(NZ):
        r.rows[6 * k : 6 * k + 6] = r.zbuf[k, 0:6].astype(F32)
    for u in range(2):
        r.wkv[core, u, y, x] = r.rows[:, u * 256 : u * 256 + 256].astype(BF16)
        r.wq[core, u, y, x] = r.rows[:, 512 + u * 128 : 640 + u * 128].astype(BF16)

    def second(ref, name, u, k):
        block = ref.at[core, u, y, x]
        return push(block, block, *sems(name, u, k), (at_y, at_x)[u](k)[1])

    def line(ref, u, turn):
        if u == 0:
            return ref.at[core, 0, :, lax.rem(x + turn, NX)]
        return ref.at[core, 1, lax.rem(y + turn, NY)]

    def third(ref, name, u, k):
        return push(line(ref, u, 0), line(ref, u, 0), *sems(name, u, k), (at_x, at_y)[u](k)[1])

    def fourth(ref, name, u, k):
        return push(line(ref, u, 4 - k), line(ref, u, 4 - k), *sems(name, u, k), partner)

    def for_all(act, *args):
        for k in (1, 3, 2):
            for u in range(2):
                act(*args, u, k)

    for_all(lambda u, k: second(r.wkv, "kv2", u, k).start())
    for_all(lambda u, k: second(r.wq, "q2", u, k).start())
    norm_frames(2)
    norm_frames(3)
    go_next(2)
    for_all(lambda u, k: second(r.wkv, "kv2", u, k).wait_recv())
    for_all(lambda u, k: third(r.wkv, "kv3", u, k).start())
    for u in range(2):
        fourth(r.wkv, "kv4", u, 0).start()
    go_next(3)
    reorder(r.normed)
    hat, lat_inverse = norm_rows(r.latents[...])
    r.lat_normed[...] = (hat * r.latent_gain[...]).astype(BF16)
    reorder(r.lat_normed)
    for_all(lambda u, k: second(r.wq, "q2", u, k).wait_recv())
    go_next(4)
    for k in (1, 3, 2):
        for u in range(2):
            third(r.wkv, "kv3", u, k).wait_recv()
            fourth(r.wkv, "kv4", u, k).start()
        if k != 2:
            go_next(5 + k // 2)
    for_all(lambda u, k: third(r.wq, "q3", u, k).start())
    for u in range(2):
        fourth(r.wq, "q4", u, 0).start()
    for k in (0, 1, 3, 2):
        for u in range(2):
            fourth(r.wkv, "kv4", u, k).wait_recv()

    def kv_proj(c, u):
        return r.wkv[c, u].reshape(WIDTH, 256)

    def q_proj(c, u):
        return r.wq[c, u].reshape(WIDTH, 128)

    for c in range(2):
        for u in range(2):
            lanes = slice(c * 512 + u * 256, c * 512 + u * 256 + 256)
            r.kv[:, lanes] = dot(r.normed[...], kv_proj(c, u)).astype(BF16)

    def slot_owner(slot):
        return ((slot >> 3) & (NZ - 1)) * NX + (slot >> 7)

    slot, lane = iota((NX * SLOTS, ROWS), 0), iota((NX * SLOTS, ROWS), 1)
    chosen = (r.route_lane[0:1] == slot_owner(slot)) & ((slot & 7) == (lane & 7))
    chosen = jnp.where(chosen, 1.0, 0.0)
    chosen_low = chosen.astype(BF16)
    alive = jnp.sum(chosen, axis=1, keepdims=True)

    def out_x(k):
        xx, to = at_x(k)
        return push(r.slots.at[xx], r.got.at[x], *sems("out_x", k), to)

    for i in range(NX):
        span = slice(i * SLOTS, i * SLOTS + SLOTS)
        r.slots[i, :, : 2 * INNER] = dot(chosen_low[span], r.kv[...]).astype(BF16)
        r.slots[i, :, 2 * INNER :] = jnp.broadcast_to(alive[span], (SLOTS, 128)).astype(BF16)
    for k in (1, 3, 2):
        out_x(k).start()
    r.got[x] = r.slots[x]
    go_next(7)
    for k in (1, 3, 2):
        for u in range(2):
            third(r.wq, "q3", u, k).wait_recv()
            fourth(r.wq, "q4", u, k).start()
    for k in (0, 1, 3, 2):
        for u in range(2):
            fourth(r.wq, "q4", u, k).wait_recv()
    query = jnp.concatenate([dot(r.lat_normed[...], q_proj(c, u)) for c in range(2) for u in range(2)], axis=1)
    r.qrow[...] = by_head((query * HEAD**-0.5).astype(BF16))
    for c in range(2):
        for u in range(2):
            lanes = slice(c * 512 + u * 256, c * 512 + u * 256 + 256)
            r.lat_kv[:, lanes] = dot(r.lat_normed[...], kv_proj(c, u)).astype(BF16)
    r.lat_scores[...] = dot_nt(r.lat_kv[:, :INNER], r.qrow[...])
    go_next(8)

    @pl.loop(0, NZ)
    def _(s):
        r.gorow[s] = by_head(r.gob[s])

    r.lat_gprob[...] = dot_nt(r.lat_kv[:, INNER:], r.gorow[z])
    for k in (1, 3, 2):
        out_x(k).wait_recv()

    got = r.got[...].reshape(NZ * KEYS, SEND)
    for i in range(4):
        span = slice(i * 128, i * 128 + 128)
        r.kvs[i * 4 : i * 4 + 4] = dot(r.sorting[span], got).astype(BF16).reshape(4, KEYS, SEND)
    r.scores[...] = dot_nt(r.kvs[:, :, :INNER].reshape(NZ * KEYS, INNER), r.qrow[...]).reshape(NZ, KEYS, INNER)

    @pl.loop(0, NZ)
    def _(s):
        live = jnp.concatenate([r.kvs[s, :, 2 * INNER :].astype(F32)] * 4, axis=1)
        scores = jnp.where(live > 0.5, r.scores[s], DEAD)
        gprob = dot_nt(r.kvs[s, :, INNER : 2 * INNER], r.gorow[s])
        top = jnp.max(scores, axis=0, keepdims=True)
        weight = jnp.exp(scores - top)
        r.scores[s] = scores
        r.gprob[s] = gprob
        r.stat[s, 0] = top
        r.stat[s, 1] = jnp.sum(weight, axis=0, keepdims=True)
        r.stat[s, 2] = jnp.sum(weight * gprob, axis=0, keepdims=True)

    def stat_to(k):
        zz, to = at_z(k)
        return push(r.stat.at[zz], r.stat_got.at[z], *sems("stat_to", k), to)

    each(1, NZ, lambda k: stat_to(k).start())
    r.stat_got[z] = r.stat[z]
    top = jnp.max(r.lat_scores[...], axis=0, keepdims=True)
    weight = jnp.exp(r.lat_scores[...] - top)
    total = jnp.sum(weight, axis=0, keepdims=True)
    mixed = jnp.sum(weight * r.lat_gprob[...], axis=0, keepdims=True)
    each(1, NZ, lambda k: stat_to(k).wait_recv())
    best = top
    for i in range(NZ):
        best = jnp.maximum(best, r.stat_got[i, 0])
    total = total * jnp.exp(top - best)
    mixed = mixed * jnp.exp(top - best)
    for i in range(NZ):
        factor = jnp.exp(r.stat_got[i, 0] - best)
        total = total + r.stat_got[i, 1] * factor
        mixed = mixed + r.stat_got[i, 2] * factor
    r.stat_own[0] = best
    r.stat_own[1] = 1.0 / total
    r.stat_own[2] = mixed / total

    def stat_from(k):
        return push(r.stat_own, r.stat_all.at[z], *sems("stat_from", k), at_z(k)[1])

    each(1, NZ, lambda k: stat_from(k).start())
    r.stat_all[z] = r.stat_own[...]

    prob = jnp.exp(r.lat_scores[...] - r.stat_own[0]) * r.stat_own[1]
    lat_low = prob.astype(BF16)
    lat_gs = (prob * (r.lat_gprob[...] - r.stat_own[2])).astype(BF16)
    r.lat_out[0] = head_blocks(lat_gs, r.lat_kv[:, :INNER])
    r.lat_out[1] = dot(lat_gs, r.qrow[...])
    r.lat_out[2] = dot(lat_low, r.gorow[z])
    r.lat_out[3] = head_blocks(lat_low, r.lat_kv[:, INNER:])
    each(1, NZ, lambda k: stat_from(k).wait_recv())

    @pl.loop(0, NZ)
    def _(s):
        prob = jnp.exp(r.scores[s] - r.stat_all[s, 0]) * r.stat_all[s, 1]
        low = prob.astype(BF16)
        r.gs[s] = (prob * (r.gprob[s] - r.stat_all[s, 2])).astype(BF16)
        r.gkv[s, :, INNER:] = dot(low, r.gorow[s]).astype(BF16)
        r.part[s] = head_blocks(low, r.kvs[s, :, INNER : 2 * INNER])

    gs = r.gs[...].reshape(NZ * KEYS, INNER)
    r.gkv[:, :, :INNER] = dot(gs, r.qrow[...]).astype(BF16).reshape(NZ, KEYS, INNER)
    gkv = r.gkv[...].reshape(NZ * KEYS, 2 * INNER)

    def back_x(k):
        xx, to = at_x(k)
        return push(r.back.at[xx], r.back_got.at[x], *sems("back_x", k), to)

    for i in range(NX):
        span = slice(i * SLOTS, i * SLOTS + SLOTS)
        r.back[i] = dot_tn(r.sorting[:, span], gkv).astype(BF16)
    for k in (1, 3, 2):
        back_x(k).start()

    def ring(way, s):
        to = at_z(1 if way == 0 else NZ - 1)[1]
        return push(r.ring_out.at[way, s], r.ring_in.at[way, s], *sems("ring", way, s), to)

    def ring_send(s):
        for way in range(2 if s < 8 else 1):
            owner = lax.rem(z + (9 - s if way == 0 else 8 + s), NZ)
            value = r.part[owner]
            if s > 1:
                value = value + r.ring_in[way, s - 1].astype(F32)
            r.ring_out[way, s] = value.astype(BF16)
            ring(way, s).start()

    def ring_wait(s):
        for way in range(2 if s < 8 else 1):
            ring(way, s).wait_recv()

    def ring_next(s):
        ring_wait(s)
        ring_send(s + 1)

    ring_send(1)
    gquery = (head_blocks(gs, r.kvs[:, :, :INNER].reshape(NZ * KEYS, INNER)) + r.lat_out[0]) * HEAD**-0.5
    own = jnp.concatenate([gquery, r.lat_out[1], r.lat_out[2]], axis=1)
    for c in range(2):
        for p in range(NP):
            for j in range(3):
                first = c * 768 + p % 2 * 384 + j * 128
                r.sums[c, p, j] = own[p // 2 * 8 : p // 2 * 8 + 8, first : first + 128]
    sum_core = push(r.sums.at[other], r.sums_core, *sems("sum_core", 0), partner)
    sum_core.start()
    ring_next(1)
    sum_core.wait_recv()

    @pl.loop(0, NP)
    def _(p):
        r.sums_core[p] = r.sums_core[p] + r.sums[core, p]

    def sum_plane(k):
        p, to = at_plane(k)
        return push(r.sums_core.at[p], r.sums_plane.at[me], *sems("sum_plane", k), to)

    each(1, NP, lambda k: sum_plane(k).start())
    r.sums_plane[me] = r.sums_core[me]
    ring_next(2)
    for k in (1, 3, 2):
        back_x(k).wait_recv()
    r.back_got[x] = r.back[x]
    ring_next(3)

    slot = iota((ROWS, NX * SLOTS), 1)
    route = jnp.concatenate([r.route_rows[...]] * 4, axis=1)
    mine = (route == slot_owner(slot)) & ((slot & 7) == (iota((ROWS, NX * SLOTS), 0) & 7))
    mine = jnp.where(mine, 1.0, 0.0).astype(BF16)
    r.kv[...] = dot(mine, r.back_got[...].reshape(NX * SLOTS, 2 * INNER)).astype(BF16)
    grad_norm = 0.0
    for c in range(2):
        for u in range(2):
            lanes = slice(c * 512 + u * 256, c * 512 + u * 256 + 256)
            grad_norm = grad_norm + dot_nt(r.kv[:, lanes], kv_proj(c, u))
    r.normed[...] = grad_norm.astype(BF16)
    for i in range(4):
        lanes = slice(i * 384, i * 384 + 384)
        natural = dot_nt(r.normed[:, lanes], r.order[...])
        term = jnp.sum(natural * r.hat[:, lanes], axis=0, keepdims=True)
        for j in range(3):
            r.media[i * 3 + j] = term[:, j * 128 : j * 128 + 128]
    for i in range(12, NP):
        r.media[i] = jnp.zeros((1, 128), F32)
    med_core = push(r.media, r.media_core, *sems("med_core", 0), partner)
    med_core.start()
    each(1, NP, lambda k: sum_plane(k).wait_recv())
    ring_next(4)
    partial = r.sums_plane[0]
    for p in range(1, NP):
        partial = partial + r.sums_plane[p]
    r.chunk[0:3] = partial
    med_core.wait_recv()

    @pl.loop(0, NP)
    def _(p):
        r.media_core[p] = r.media_core[p] + r.media[p]

    def med_plane(k):
        p, to = at_plane(k)
        return push(r.media_core.at[p], r.media_plane.at[me], *sems("med_plane", k), to)

    each(1, NP, lambda k: med_plane(k).start())
    r.media_plane[me] = r.media_core[me]

    def red_z(j):
        return push(r.chunk.at[j], r.chunk_got.at[j, z], *sems("red_z", j, z), device(y, core, 4 * j, x))

    def red_z_in(j, k):
        sender = lax.rem(4 * j + k, NZ)
        return push(r.chunk.at[j], r.chunk_got.at[j, sender], *sems("red_z", j, sender), device(y, core, 4 * j, x))

    def reduce_start(j):
        @pl.when(z != 4 * j)
        def _():
            red_z(j).start()

        @pl.when(z == 4 * j)
        def _():
            r.chunk_got[j, 4 * j] = r.chunk[j]

    def all_z(j, k):
        tile = r.whole.at[core, me, j]
        return push(tile, tile, *sems("all_z", j, k), device(y, core, lax.rem(4 * j + k, NZ), x))

    def all_z_in(j):
        k = lax.rem(z + NZ - 4 * j, NZ)
        tile = r.whole.at[core, me, j]
        return push(tile, tile, *sems("all_z", j, k), device(y, core, lax.rem(4 * j + 1, NZ), x))

    def reduce_end(j):
        @pl.when(z == 4 * j)
        def _():
            each(1, NZ, lambda k: red_z_in(j, k).wait_recv())
            value = r.chunk_got[j, 0]
            for i in range(1, NZ):
                value = value + r.chunk_got[j, i]
            r.whole[core, me, j] = value
            each(1, NZ, lambda k: all_z(j, k).start())

    for j in range(3):
        reduce_start(j)
    each(1, NP, lambda k: med_plane(k).wait_recv())
    partial = r.media_plane[0]
    for p in range(1, NP):
        partial = partial + r.media_plane[p]
    r.chunk[3] = jnp.broadcast_to(partial, (8, 128))
    reduce_start(3)
    ring_next(5)
    for j in range(4):
        reduce_end(j)
    ring_next(6)
    for j in range(4):
        @pl.when(z != 4 * j)
        def _():
            all_z_in(j).wait_recv()

    def all_plane(k):
        block = r.whole.at[core, me]
        return push(block, block, *sems("all_plane", k), at_plane(k)[1])

    def all_core(p):
        block = r.whole.at[core, p]
        return push(block, block, *sems("all_core", p), partner)

    each(1, NP, lambda k: all_plane(k).start())
    all_core(me).start()
    ring_next(7)

    def forward(k):
        all_plane(k).wait_recv()
        all_core(lax.rem(me + NP - k, NP)).start()

    each(1, NP, forward)
    ring_wait(8)
    r.attended[...] = (
        r.part[z] + r.lat_out[3] + r.ring_in[0, 8].astype(F32) + r.ring_in[1, 7].astype(F32)
    ).astype(BF16)
    each(0, NP, lambda p: all_core(p).wait_recv())

    def gathered(c, rows, g, j):
        return r.whole[c, rows * 2 + g, j]

    strips = []
    for c in range(2):
        for g in range(2):
            for j in range(3):
                strips.append(jnp.concatenate([gathered(c, rows, g, j) for rows in range(8)], axis=0))

    def precise(values, weight):
        high = values.astype(BF16)
        low = (values - high.astype(F32)).astype(BF16)
        result = dot_nt(jnp.concatenate([high, low], axis=0), weight)
        return result[:LAT] + result[LAT:]

    grad = 0.0
    for i in range(4):
        grad = grad + precise(strips[i], q_proj(i // 2, i % 2))
        both = jnp.concatenate([strips[4 + 2 * i], strips[5 + 2 * i]], axis=1)
        grad = grad + precise(both, kv_proj(i // 2, i % 2))
    natural = []
    for i in range(4):
        rest = grad[:, i * 384 : i * 384 + 384]
        pieces = []
        for _ in range(3):
            piece = rest.astype(BF16)
            rest = rest - piece.astype(F32)
            pieces.append(piece)
        moved = dot_nt(jnp.concatenate(pieces, axis=0), r.order[...])
        natural.append(moved[:LAT] + moved[LAT : 2 * LAT] + moved[2 * LAT :])
    grad = jnp.concatenate(natural, axis=1)
    hat, lat_inverse = norm_rows(r.latents[...])
    r.latent_gain_grad[...] = jnp.sum(grad * hat, axis=0, keepdims=True)
    grad_hat = grad * r.latent_gain[...]
    r.latent_grad[...] = lat_inverse * (
        grad_hat
        - jnp.mean(grad_hat, -1, keepdims=True)
        - hat * jnp.mean(grad_hat * hat, -1, keepdims=True)
    )
    for p in range(12):
        r.media_gain_grad[:, p * 128 : p * 128 + 128] = r.whole[core, p, 3][0:1]

    each(1, NZ, lambda k: along_z(k).wait_send())
    for s in range(1, 9):
        for way in range(2 if s < 8 else 1):
            go(way, s).wait_send()
            ring(way, s).wait_send()
    for ref, name in ((r.wkv, "kv"), (r.wq, "q")):
        for u in range(2):
            for k in range(4):
                if k:
                    second(ref, name + "2", u, k).wait_send()
                    third(ref, name + "3", u, k).wait_send()
                fourth(ref, name + "4", u, k).wait_send()
    for k in range(1, 4):
        out_x(k).wait_send()
        back_x(k).wait_send()
    each(1, NZ, lambda k: stat_to(k).wait_send())
    each(1, NZ, lambda k: stat_from(k).wait_send())
    sum_core.wait_send()
    med_core.wait_send()
    each(1, NP, lambda k: sum_plane(k).wait_send())
    each(1, NP, lambda k: med_plane(k).wait_send())
    for j in range(4):
        @pl.when(z != 4 * j)
        def _():
            red_z(j).wait_send()

        @pl.when(z == 4 * j)
        def _():
            each(1, NZ, lambda k: all_z(j, k).wait_send())
    each(1, NP, lambda k: all_plane(k).wait_send())
    each(0, NP, lambda p: all_core(p).wait_send())


def body(frame_features, frame_owner, latents, latent_gain, media_gain, query_proj, keyval_proj, grad_output):
    half = INNER // 2
    shard = jnp.stack(
        [
            jnp.concatenate([keyval_proj[:, :INNER], query_proj[:, :half]], axis=1),
            jnp.concatenate([keyval_proj[:, INNER:], query_proj[:, half:]], axis=1),
        ]
    )
    shard = jnp.pad(shard, ((0, 0), (0, 5), (0, 0)))
    route = jnp.repeat(frame_owner[0, :, 0], TOK)
    scratch = [pltpu.VMEM(*spec) for spec in BUFFERS.values()]
    scratch += [DMA(shape) for shape in SEMS.values() for _ in range(2)]
    vmem = pl.BlockSpec(memory_space=pltpu.VMEM)
    attended, latent_grad, latent_gain_grad, media_gain_grad = pl.pallas_call(
        kernel,
        out_shape=(
            jax.ShapeDtypeStruct((LAT, INNER), BF16),
            jax.ShapeDtypeStruct((LAT, WIDTH), F32),
            jax.ShapeDtypeStruct((1, WIDTH), F32),
            jax.ShapeDtypeStruct((1, WIDTH), F32),
        ),
        in_specs=[vmem] * len(INPUTS),
        out_specs=(vmem,) * 4,
        scratch_shapes=scratch,
        compiler_params=pltpu.CompilerParams(collective_id=0, has_side_effects=True, vmem_limit_bytes=60 << 20),
        name="resampler",
    )(
        shard,
        frame_features.reshape(ROWS, WIDTH),
        latents,
        latent_gain.reshape(1, WIDTH),
        media_gain.reshape(1, WIDTH),
        jnp.broadcast_to(route[None, :], (8, ROWS)),
        jnp.broadcast_to(route[:, None], (ROWS, 128)),
        grad_output[0, 0],
        jnp.asarray(gathered_order(), BF16),
        jnp.asarray(sample_order(), BF16),
    )
    return (attended[None, None], latent_grad, latent_gain_grad[0], media_gain_grad[0])


def solution(mesh):
    placed = (
        P("dp", "frame", None, None),
        P("dp", "frame", None),
        P(),
        P(),
        P(),
        P(("dp", "frame"), None),
        P(("dp", "frame"), None),
        P("dp", "frame", None, None),
    )
    return jax.shard_map(
        body,
        mesh=mesh,
        in_specs=placed,
        out_specs=(P("dp", "frame", None, None), P(), P(), P()),
        check_vma=False,
    )
```

```python
import jax
import jax.numpy as jnp
from jax import lax
from jax.experimental import pallas as pl
from jax.experimental.pallas import tpu as pltpu
from jax.sharding import PartitionSpec as P

NX, NY, NZ = 4, 4, 16
NP = NX * NY
HEADS, HEAD, INNER, WIDTH, LAT = 8, 64, 512, 1536, 64
TOK, FRAMES = 8, 32
ROWS = FRAMES * TOK
KEYS = NX * TOK
SLOTS = NZ * TOK
SEND = 2 * INNER + 128
DEAD = -1e30
MESH = pl.DeviceIdType.MESH
F32, BF16 = jnp.float32, jnp.bfloat16
DMA = pltpu.SemaphoreType.DMA


def dot(left, right, dims=((1,), (0,))):
    return lax.dot_general(left, right, (dims, ((), ())), preferred_element_type=F32)


def dot_nt(left, right):
    return dot(left, right, ((1,), (1,)))


def dot_tn(left, right):
    return dot(left, right, ((0,), (0,)))


def norm_rows(values):
    center = values - jnp.mean(values, -1, keepdims=True)
    inverse = lax.rsqrt(jnp.mean(center * center, -1, keepdims=True) + 1e-05)
    return center * inverse, inverse


def iota(shape, dim):
    return lax.broadcasted_iota(jnp.int32, shape, dim)


def gathered_order():
    place = iota((384, 384), 1)
    block = (place >= 96).astype(jnp.int32) + (place >= 192).astype(jnp.int32) + (place >= 288).astype(jnp.int32)
    inner = place - block * 96
    six = (inner * 43) >> 8
    last = inner - six * 6
    odd = (last >= 3).astype(jnp.int32)
    natural = odd * 192 + six * 12 + block * 3 + last - odd * 3
    return jnp.where(iota((384, 384), 0) == natural, 1.0, 0.0).astype(BF16)


def sample_order():
    shape = (NZ * KEYS, NZ * KEYS)
    place = iota(shape, 0)
    source = (((place >> 3) & 3) << 7) + ((place >> 5) << 3) + (place & 7)
    return jnp.where(iota(shape, 1) == source, 1.0, 0.0).astype(BF16)


def source_order():
    shape = (NZ * KEYS, NZ * KEYS)
    place = iota(shape, 0)
    sample = (((place >> 3) & (NZ - 1)) << 5) + ((place >> 7) << 3) + (place & 7)
    return jnp.where(iota(shape, 1) == sample, 1.0, 0.0).astype(BF16)


def by_head(ref, rows):
    for head in range(HEADS):
        lanes = slice(head // 2 * 128, head // 2 * 128 + 128)
        own = (iota((LAT, 128), 1) >> 6) == head % 2
        part = jnp.where(own, rows[:, lanes].astype(F32), 0.0).astype(BF16)
        ref[head * LAT : head * LAT + LAT, lanes] = part


def head_blocks(left, right):
    blocks = []
    for pair in range(HEADS // 2):
        lanes = slice(pair * 128, pair * 128 + 128)
        both = dot_tn(left[:, lanes], right[:, lanes])
        blocks.append(jnp.where(iota((HEAD, 128), 1) < HEAD, both[:HEAD], both[HEAD:]))
    return jnp.concatenate(blocks, axis=1)


def push(src, dst, send, recv, to):
    return pltpu.make_async_remote_copy(
        src_ref=src, dst_ref=dst, send_sem=send, recv_sem=recv, device_id=to, device_id_type=MESH
    )


INPUTS = ("keyval", "query", "frames", "latents", "latent_gain", "media_gain", "route", "grad")
OUTPUTS = ("attended", "latent_grad", "lat_inverse", "latent_gain_grad", "media_gain_grad")
BUFFERS = dict(
    order=((384, 384), BF16),
    sorting=((NZ * KEYS, NZ * KEYS), BF16),
    resorting=((NZ * KEYS, NZ * KEYS), BF16),
    low=((NZ, KEYS, INNER), BF16),
    shard=((2, 8, 768), BF16),
    pair=((2, 8, 768), BF16),
    pair_rows=((8, 768), F32),
    zkv=((NZ, 8, 512), BF16),
    zq=((NZ, 8, 256), BF16),
    rows=((6 * NZ, 768), F32),
    wkv=((2, 2, NY, NX, 6 * NZ, 256), BF16),
    wq=((2, 2, NY, NX, 6 * NZ, 128), BF16),
    gob=((NZ, LAT, INNER), BF16),
    hat=((ROWS, WIDTH), F32),
    normed=((ROWS, WIDTH), BF16),
    kv=((ROWS, SEND), BF16),
    mine=((ROWS, NX * SLOTS), BF16),
    slots=((NX, SLOTS, SEND), BF16),
    got=((NX, SLOTS, SEND), BF16),
    kvs=((NZ, KEYS, SEND), BF16),
    lat_normed=((LAT, WIDTH), BF16),
    lat_kv=((LAT, 2 * INNER), BF16),
    qrow=((HEADS * LAT, INNER), BF16),
    gorow=((NZ, HEADS * LAT, INNER), BF16),
    scores=((NZ, KEYS, INNER), F32),
    gprob=((NZ, KEYS, INNER), F32),
    lat_scores=((LAT, INNER), F32),
    lat_gprob=((LAT, INNER), F32),
    stat=((NZ, 2, 1, INNER), F32),
    stat_got=((NZ, 2, 1, INNER), F32),
    stat_own=((2, 1, INNER), F32),
    stat_all=((NZ, 2, 1, INNER), F32),
    gs=((NZ, KEYS, INNER), BF16),
    gkv=((NZ, KEYS, 2 * INNER), BF16),
    back=((NX, SLOTS, 2 * INNER), BF16),
    back_got=((NX, SLOTS, 2 * INNER), BF16),
    lat_out=((4, LAT, INNER), F32),
    part=((4, 4, LAT, INNER), BF16),
    near_in=((3, 4, LAT, INNER), BF16),
    far_out=((4, LAT, INNER), BF16),
    far_in=((4, LAT, INNER), BF16),
    own_part=((LAT, INNER), F32),
    sums=((2, NP, 3, 8, 128), F32),
    sums_core=((NP, 3, 8, 128), F32),
    sums_plane=((NP, 3, 8, 128), F32),
    chunk=((3, 8, 128), F32),
    sum_quads=((4, 3, 8, 128), F32),
    sum_class=((4, 3, 8, 128), F32),
    whole=((2, NP, 3, 8, 128), F32),
    media=((12, 1, 128), F32),
    media_core=((12, 1, 128), F32),
    med_quads=((4, 12, 1, 128), F32),
    med_class=((4, 12, 1, 128), F32),
    med_whole=((NP, 12, 1, 128), F32),
)
SEMS = dict(
    swap=(1,), along_z=(NZ,), along_q=(NZ,), go_far=(4,), go_near=(4, 3), kv2=(2, 4), kv3=(2, 4), kv4=(2, 4), q2=(2, 4), q3=(2, 4), q4=(2, 4),
    out_x=(4,), back_x=(4,), stat_to=(NZ,), stat_from=(NZ,), near=(3,), far=(4,), sum_core=(1,), sum_plane=(NP,),
    med_core=(1,), sum_far=(4,), sum_near=(3,), med_far=(4,), med_near=(3,), all_plane=(NP,), all_core=(NP,), med_all=(NP,),
)
NEAR = (1, NZ - 1, 2)


class Refs:
    pass


def kernel(*refs):
    r = Refs()
    names = INPUTS + OUTPUTS + tuple(BUFFERS) + tuple(n + e for n in SEMS for e in ("_s", "_r"))
    for name, ref in zip(names, refs, strict=True):
        setattr(r, name, ref)

    def sems(name, *at):
        return getattr(r, name + "_s").at[at], getattr(r, name + "_r").at[at]

    dp, fr = lax.axis_index("dp"), lax.axis_index("frame")
    y, core, z, x = lax.div(dp, 2), lax.rem(dp, 2), lax.div(fr, NX), lax.rem(fr, NX)
    other, me = 1 - core, y * NX + x

    def device(yy, cc, zz, xx):
        return (yy * 2 + cc, zz * NX + xx)

    partner = device(y, other, z, x)

    def at_z(k):
        zz = lax.rem(z + k, NZ)
        return zz, device(y, core, zz, x)

    def at_x(k):
        xx = lax.rem(x + k, NX)
        return xx, device(y, core, z, xx)

    def at_y(k):
        yy = lax.rem(y + k, NY)
        return yy, device(yy, core, z, x)

    def at_plane(k):
        p = lax.rem(me + k, NP)
        return p, device(lax.div(p, NX), core, z, lax.rem(p, NX))

    def each(lo, hi, act):
        @pl.loop(lo, hi)
        def _(k):
            act(k)

    barrier = pltpu.get_barrier_semaphore()

    def greet(to):
        pl.semaphore_signal(barrier, inc=1, device_id=to, device_id_type=MESH)

    each(1, NZ, lambda k: greet(at_z(k)[1]))
    each(1, NP, lambda k: greet(at_plane(k)[1]))
    greet(partner)
    r.gob[z] = r.grad[...]
    r.pair_rows[...] = jnp.zeros_like(r.pair_rows)
    for c in range(2):
        r.pair_rows[0:3, 0:512] = r.keyval[:, c * 512 : c * 512 + 512].astype(F32)
        r.pair_rows[0:3, 512:768] = r.query[:, c * 256 : c * 256 + 256].astype(F32)
        r.shard[c] = r.pair_rows[...].astype(BF16)
    r.pair[core] = r.shard[core]
    media_gain = r.media_gain[...].reshape(1, WIDTH)
    latent_gain = r.latent_gain[...].reshape(1, WIDTH)

    @pl.loop(0, ROWS // 32)
    def _(b):
        span = pl.ds(pl.multiple_of(b * 32, 32), 32)
        hat, _ = norm_rows(r.frames[span, :].astype(F32))
        r.hat[span, :] = hat
        r.normed[span, :] = (hat * media_gain).astype(BF16)

    def reorder(ref):
        for i in range(4):
            lanes = slice(i * 384, i * 384 + 384)
            ref[:, lanes] = dot(ref[:, lanes], r.order[...]).astype(BF16)

    r.order[...] = gathered_order()
    r.sorting[...] = sample_order()
    r.resorting[...] = source_order()
    r.qrow[...] = jnp.zeros_like(r.qrow)

    @pl.loop(0, NZ)
    def _(s):
        r.gorow[s] = jnp.zeros((HEADS * LAT, INNER), BF16)

    reorder(r.normed)
    hat, _ = norm_rows(r.latents[...])
    r.lat_normed[...] = (hat * latent_gain).astype(BF16)
    reorder(r.lat_normed)
    def slot_owner(slot):
        return ((slot >> 3) & (NZ - 1)) * NX + (slot >> 7)

    slot = iota((ROWS, NX * SLOTS), 1)
    route = jnp.concatenate([r.route[...]] * 4, axis=1)
    mine = (route == slot_owner(slot)) & ((slot & 7) == (iota((ROWS, NX * SLOTS), 0) & 7))
    r.mine[...] = jnp.where(mine, 1.0, 0.0).astype(BF16)
    r.kv[:, 2 * INNER :] = jnp.ones((ROWS, 128), BF16)
    pl.semaphore_wait(barrier, NZ - 1 + NP - 1 + 1)

    swap = push(r.shard.at[other], r.pair.at[core], *sems("swap", 0), partner)
    swap.start()

    def go_far(j):
        return push(r.gob.at[z], r.gob.at[z], *sems("go_far", j), at_z(4 * j)[1])

    def go_near(i, d):
        block = r.gob.at[lax.rem(z + 4 * i, NZ)]
        return push(block, block, *sems("go_near", i, d), at_z(NEAR[d])[1])

    swap.wait()
    r.pair_rows[...] = jnp.zeros_like(r.pair_rows)
    r.pair_rows[0:3] = r.pair[0, 0:3].astype(F32)
    r.pair_rows[3:6] = r.pair[1, 0:3].astype(F32)
    r.zkv[z] = r.pair_rows[:, :512].astype(BF16)
    r.zq[z] = r.pair_rows[:, 512:].astype(BF16)

    def along_z(k):
        return push(r.zkv.at[z], r.zkv.at[z], *sems("along_z", k), at_z(k)[1])

    def along_q(k):
        return push(r.zq.at[z], r.zq.at[z], *sems("along_q", k), at_z(k)[1])

    each(1, NZ, lambda k: along_z(k).start())
    each(1, NZ, lambda k: along_q(k).start())
    each(1, NZ, lambda k: along_z(k).wait_recv())
    for k in range(NZ):
        r.rows[6 * k : 6 * k + 6, :512] = r.zkv[k, 0:6].astype(F32)
    for u in range(2):
        r.wkv[core, u, y, x] = r.rows[:, u * 256 : u * 256 + 256].astype(BF16)

    def second(ref, name, u, k):
        block = ref.at[core, u, y, x]
        return push(block, block, *sems(name, u, k), (at_y, at_x)[u](k)[1])

    def line(ref, u, turn):
        if u == 0:
            return ref.at[core, 0, :, lax.rem(x + turn, NX)]
        return ref.at[core, 1, lax.rem(y + turn, NY)]

    def third(ref, name, u, k):
        return push(line(ref, u, 0), line(ref, u, 0), *sems(name, u, k), (at_x, at_y)[u](k)[1])

    def fourth(ref, name, u, k):
        return push(line(ref, u, 4 - k), line(ref, u, 4 - k), *sems(name, u, k), partner)

    def for_all(act, *args):
        for k in (1, 3, 2):
            for u in range(2):
                act(*args, u, k)

    for_all(lambda u, k: second(r.wkv, "kv2", u, k).start())
    each(1, NZ, lambda k: along_q(k).wait_recv())
    for k in range(NZ):
        r.rows[6 * k : 6 * k + 6, 512:] = r.zq[k, 0:6].astype(F32)
    for u in range(2):
        r.wq[core, u, y, x] = r.rows[:, 512 + u * 128 : 640 + u * 128].astype(BF16)
    for_all(lambda u, k: second(r.wq, "q2", u, k).start())
    for j in (2, 1, 3):
        go_far(j).start()
    for d in range(3):
        go_near(0, d).start()
    for_all(lambda u, k: second(r.wkv, "kv2", u, k).wait_recv())
    for_all(lambda u, k: third(r.wkv, "kv3", u, k).start())
    for u in range(2):
        fourth(r.wkv, "kv4", u, 0).start()
    for_all(lambda u, k: second(r.wq, "q2", u, k).wait_recv())
    for k in (1, 3, 2):
        for u in range(2):
            third(r.wkv, "kv3", u, k).wait_recv()
            fourth(r.wkv, "kv4", u, k).start()
    for_all(lambda u, k: third(r.wq, "q3", u, k).start())
    for u in range(2):
        fourth(r.wq, "q4", u, 0).start()
    for j in (1, 3, 2):
        go_far(j).wait_recv()
        for d in range(3):
            go_near(4 - j, d).start()
    for k in (0, 1, 3, 2):
        for u in range(2):
            fourth(r.wkv, "kv4", u, k).wait_recv()

    def kv_proj(c, u):
        return r.wkv[c, u].reshape(WIDTH, 256)

    def q_proj(c, u):
        return r.wq[c, u].reshape(WIDTH, 128)

    for c in range(2):
        for u in range(2):
            lanes = slice(c * 512 + u * 256, c * 512 + u * 256 + 256)
            r.kv[:, lanes] = dot(r.normed[...], kv_proj(c, u)).astype(BF16)

    def out_x(k):
        xx, to = at_x(k)
        return push(r.slots.at[xx], r.got.at[x], *sems("out_x", k), to)

    for i in range(NX):
        span = slice(i * SLOTS, i * SLOTS + SLOTS)
        r.slots[i] = dot_tn(r.mine[:, span], r.kv[...]).astype(BF16)
    for k in (1, 3, 2):
        out_x(k).start()
    r.got[x] = r.slots[x]
    for k in (1, 3, 2):
        for u in range(2):
            third(r.wq, "q3", u, k).wait_recv()
            fourth(r.wq, "q4", u, k).start()
    for k in (0, 1, 3, 2):
        for u in range(2):
            fourth(r.wq, "q4", u, k).wait_recv()
    query = jnp.concatenate([dot(r.lat_normed[...], q_proj(c, u)) for c in range(2) for u in range(2)], axis=1)
    by_head(r.qrow, (query * HEAD**-0.5).astype(BF16))
    for c in range(2):
        for u in range(2):
            lanes = slice(c * 512 + u * 256, c * 512 + u * 256 + 256)
            r.lat_kv[:, lanes] = dot(r.lat_normed[...], kv_proj(c, u)).astype(BF16)
    r.lat_scores[...] = dot_nt(r.lat_kv[:, :INNER], r.qrow[...])
    for i in range(4):
        for d in range(3):
            go_near(i, d).wait_recv()

    @pl.loop(0, NZ, unroll=2)
    def _(s):
        by_head(r.gorow.at[s], r.gob[s])

    r.lat_gprob[...] = dot_nt(r.lat_kv[:, INNER:], r.gorow[z])
    for k in (1, 3, 2):
        out_x(k).wait_recv()

    got = r.got[...].reshape(NZ * KEYS, SEND)
    for i in range(4):
        span = slice(i * 128, i * 128 + 128)
        r.kvs[i * 4 : i * 4 + 4] = dot(r.sorting[span], got).astype(BF16).reshape(4, KEYS, SEND)
    r.scores[...] = dot_nt(r.kvs[:, :, :INNER].reshape(NZ * KEYS, INNER), r.qrow[...]).reshape(NZ, KEYS, INNER)

    @pl.loop(0, NZ, unroll=4)
    def _(s):
        live = jnp.concatenate([r.kvs[s, :, 2 * INNER :].astype(F32)] * 4, axis=1)
        scores = jnp.where(live > 0.5, r.scores[s], DEAD)
        gprob = dot_nt(r.kvs[s, :, INNER : 2 * INNER], r.gorow[s])
        top = jnp.max(scores, axis=0, keepdims=True)
        weight = jnp.exp(scores - top)
        r.scores[s] = scores
        r.gprob[s] = gprob
        total = jnp.sum(weight, axis=0, keepdims=True)
        r.stat[s, 0] = top + jnp.log(total)
        r.stat[s, 1] = jnp.sum(weight * gprob, axis=0, keepdims=True) / total

    def stat_to(k):
        zz, to = at_z(k)
        return push(r.stat.at[zz], r.stat_got.at[z], *sems("stat_to", k), to)

    each(1, NZ, lambda k: stat_to(k).start())
    r.stat_got[z] = r.stat[z]
    top = jnp.max(r.lat_scores[...], axis=0, keepdims=True)
    weight = jnp.exp(r.lat_scores[...] - top)
    total = jnp.sum(weight, axis=0, keepdims=True)
    mixed = jnp.sum(weight * r.lat_gprob[...], axis=0, keepdims=True)
    each(1, NZ, lambda k: stat_to(k).wait_recv())
    best = top
    for i in range(NZ):
        best = jnp.maximum(best, r.stat_got[i, 0])
    total = total * jnp.exp(top - best)
    mixed = mixed * jnp.exp(top - best)
    for i in range(NZ):
        factor = jnp.exp(r.stat_got[i, 0] - best)
        total = total + factor
        mixed = mixed + r.stat_got[i, 1] * factor
    r.stat_own[0] = best + jnp.log(total)
    r.stat_own[1] = mixed / total

    def stat_from(k):
        return push(r.stat_own, r.stat_all.at[z], *sems("stat_from", k), at_z(k)[1])

    each(1, NZ, lambda k: stat_from(k).start())
    r.stat_all[z] = r.stat_own[...]

    prob = jnp.exp(r.lat_scores[...] - r.stat_own[0])
    lat_low = prob.astype(BF16)
    lat_gs = (prob * (r.lat_gprob[...] - r.stat_own[1])).astype(BF16)
    r.lat_out[0] = head_blocks(lat_gs, r.lat_kv[:, :INNER])
    r.lat_out[1] = dot(lat_gs, r.qrow[...])
    r.lat_out[2] = dot(lat_low, r.gorow[z])
    r.lat_out[3] = head_blocks(lat_low, r.lat_kv[:, INNER:])
    each(1, NZ, lambda k: stat_from(k).wait_recv())

    @pl.loop(0, NZ, unroll=4)
    def _(s):
        prob = jnp.exp(r.scores[s] - r.stat_all[s, 0])
        low = prob.astype(BF16)
        r.gs[s] = (prob * (r.gprob[s] - r.stat_all[s, 1])).astype(BF16)
        r.gkv[s, :, INNER:] = dot(low, r.gorow[s]).astype(BF16)
        r.low[s] = low

    gs = r.gs[...].reshape(NZ * KEYS, INNER)
    r.gkv[:, :, :INNER] = dot(gs, r.qrow[...]).astype(BF16).reshape(NZ, KEYS, INNER)
    gkv = r.gkv[...].reshape(NZ * KEYS, 2 * INNER)

    def back_x(k):
        xx, to = at_x(k)
        return push(r.back.at[xx], r.back_got.at[x], *sems("back_x", k), to)

    for i in range(NX):
        span = slice(i * SLOTS, i * SLOTS + SLOTS)
        r.back[i] = dot(r.resorting[span], gkv).astype(BF16)
    for k in (1, 3, 2):
        back_x(k).start()

    def near(d):
        return push(r.part.at[lax.rem(z + NEAR[d], 4)], r.near_in.at[d], *sems("near", d), at_z(NEAR[d])[1])

    def far(i):
        return push(r.far_out.at[lax.rem(lax.div(z, 4) + i, 4)], r.far_in.at[i], *sems("far", i), at_z(4 * i)[1])

    @pl.loop(0, NZ, unroll=4)
    def _(s):
        r.part[s & 3, s >> 2] = head_blocks(r.low[s], r.kvs[s, :, INNER : 2 * INNER]).astype(BF16)

    for d in range(3):
        near(d).start()
    gquery = (head_blocks(gs, r.kvs[:, :, :INNER].reshape(NZ * KEYS, INNER)) + r.lat_out[0]) * HEAD**-0.5
    own = jnp.concatenate([gquery, r.lat_out[1], r.lat_out[2]], axis=1)
    for c in range(2):
        for p in range(NP):
            for j in range(3):
                first = c * 768 + p % 2 * 384 + j * 128
                r.sums[c, p, j] = own[p // 2 * 8 : p // 2 * 8 + 8, first : first + 128]
    sum_core = push(r.sums.at[other], r.sums_core, *sems("sum_core", 0), partner)
    sum_core.start()
    sum_core.wait_recv()

    @pl.loop(0, NP)
    def _(p):
        r.sums_core[p] = r.sums_core[p] + r.sums[core, p]

    def sum_plane(k):
        p, to = at_plane(k)
        return push(r.sums_core.at[p], r.sums_plane.at[me], *sems("sum_plane", k), to)

    each(1, NP, lambda k: sum_plane(k).start())
    r.sums_plane[me] = r.sums_core[me]
    for k in (1, 3, 2):
        back_x(k).wait_recv()
    r.back_got[x] = r.back[x]

    r.kv[:, : 2 * INNER] = dot(r.mine[...], r.back_got[...].reshape(NX * SLOTS, 2 * INNER)).astype(BF16)
    grad_norm = 0.0
    for c in range(2):
        for u in range(2):
            lanes = slice(c * 512 + u * 256, c * 512 + u * 256 + 256)
            grad_norm = grad_norm + dot_nt(r.kv[:, lanes], kv_proj(c, u))
    r.normed[...] = grad_norm.astype(BF16)
    for i in range(4):
        lanes = slice(i * 384, i * 384 + 384)
        natural = dot_nt(r.normed[:, lanes], r.order[...])
        term = jnp.sum(natural * r.hat[:, lanes], axis=0, keepdims=True)
        for j in range(3):
            r.media[i * 3 + j] = term[:, j * 128 : j * 128 + 128]
    med_core = push(r.media, r.media_core, *sems("med_core", 0), partner)
    med_core.start()
    each(1, NP, lambda k: sum_plane(k).wait_recv())
    partial = r.sums_plane[0]
    for p in range(1, NP):
        partial = partial + r.sums_plane[p]
    r.chunk[...] = partial

    def z_far(src, got, name, j):
        return push(src, got.at[lax.div(z, 4)], *sems(name, j), at_z(4 * j)[1])

    def z_near(got, name, d):
        block = got.at[lax.rem(z, 4)]
        return push(block, block, *sems(name, d), at_z(NEAR[d])[1])

    def four(ref):
        return ref[0] + ref[1] + ref[2] + ref[3]

    def sum_far(j):
        return z_far(r.chunk, r.sum_quads, "sum_far", j)

    def sum_near(d):
        return z_near(r.sum_class, "sum_near", d)

    def med_far(j):
        return z_far(r.media_core, r.med_quads, "med_far", j)

    def med_near(d):
        return z_near(r.med_class, "med_near", d)

    for j in (2, 1, 3):
        sum_far(j).start()
    r.sum_quads[lax.div(z, 4)] = r.chunk[...]
    med_core.wait_recv()

    r.media_core[...] = r.media_core[...] + r.media[...]

    for j in (2, 1, 3):
        med_far(j).start()
    r.med_quads[lax.div(z, 4)] = r.media_core[...]
    for j in range(1, 4):
        sum_far(j).wait_recv()
    r.sum_class[lax.rem(z, 4)] = four(r.sum_quads)
    for d in range(3):
        sum_near(d).start()
    for d in range(3):
        near(d).wait_recv()
    for j in range(4):
        value = r.part[lax.rem(z, 4), j].astype(F32)
        for d in range(3):
            value = value + r.near_in[d, j].astype(F32)
        r.far_out[j] = value.astype(BF16)

        @pl.when(lax.div(z, 4) == j)
        def _():
            r.own_part[...] = value

    for i in range(1, 4):
        far(i).start()
    def all_plane(k):
        block = r.whole.at[core, me]
        return push(block, block, *sems("all_plane", k), at_plane(k)[1])

    def all_core(p):
        block = r.whole.at[core, p]
        return push(block, block, *sems("all_core", p), partner)

    def med_all(k):
        block = r.med_whole.at[me]
        return push(block, block, *sems("med_all", k), at_plane(k)[1])

    for j in range(1, 4):
        med_far(j).wait_recv()
    r.med_class[lax.rem(z, 4)] = four(r.med_quads)
    for d in range(3):
        med_near(d).start()
    for d in range(3):
        sum_near(d).wait_recv()
    r.whole[core, me] = four(r.sum_class)
    each(1, NP, lambda k: all_plane(k).start())
    all_core(me).start()
    for d in range(3):
        med_near(d).wait_recv()
    r.med_whole[me] = four(r.med_class)
    each(1, NP, lambda k: med_all(k).start())

    def forward(k):
        all_plane(k).wait_recv()
        all_core(lax.rem(me + NP - k, NP)).start()

    each(1, NP, forward)
    each(0, NP, lambda p: all_core(p).wait_recv())

    def gathered(c, rows, g, j):
        return r.whole[c, rows * 2 + g, j]

    strips = []
    for c in range(2):
        for g in range(2):
            for j in range(3):
                strips.append(jnp.concatenate([gathered(c, rows, g, j) for rows in range(8)], axis=0))

    def precise(values, weight):
        high = values.astype(BF16)
        low = (values - high.astype(F32)).astype(BF16)
        result = dot_nt(jnp.concatenate([high, low], axis=0), weight)
        return result[:LAT] + result[LAT:]

    grad = 0.0
    for i in range(4):
        grad = grad + precise(strips[i], q_proj(i // 2, i % 2))
        both = jnp.concatenate([strips[4 + 2 * i], strips[5 + 2 * i]], axis=1)
        grad = grad + precise(both, kv_proj(i // 2, i % 2))
    natural = []
    for i in range(4):
        rest = grad[:, i * 384 : i * 384 + 384]
        pieces = []
        for _ in range(3):
            high = rest.astype(BF16)
            rest = rest - high.astype(F32)
            pieces.append(high)
        moved = dot_nt(jnp.concatenate(pieces, axis=0), r.order[...])
        natural.append(moved[:LAT] + moved[LAT : 2 * LAT] + moved[2 * LAT :])
    grad = jnp.concatenate(natural, axis=1)
    hat, inverse = norm_rows(r.latents[...])
    r.latent_gain_grad[...] = jnp.sum(grad * hat, axis=0, keepdims=True)
    grad_hat = grad * latent_gain
    r.latent_grad[...] = (
        grad_hat
        - jnp.mean(grad_hat, -1, keepdims=True)
        - hat * jnp.mean(grad_hat * hat, -1, keepdims=True)
    )
    r.lat_inverse[...] = jnp.broadcast_to(inverse, (LAT, 128))
    value = r.own_part[...] + r.lat_out[3]
    for i in range(1, 4):
        far(i).wait_recv()
        value = value + r.far_in[i].astype(F32)
    r.attended[...] = value
    each(1, NP, lambda k: med_all(k).wait_recv())
    value = r.med_whole[0]
    for p in range(1, NP):
        value = value + r.med_whole[p]
    for i in range(12):
        r.media_gain_grad[:, i * 128 : i * 128 + 128] = value[i]

    each(1, NZ, lambda k: along_z(k).wait_send())
    each(1, NZ, lambda k: along_q(k).wait_send())
    for j in range(1, 4):
        go_far(j).wait_send()
        far(j).wait_send()
    for d in range(3):
        near(d).wait_send()
        for i in range(4):
            go_near(i, d).wait_send()
    for ref, name in ((r.wkv, "kv"), (r.wq, "q")):
        for u in range(2):
            for k in range(4):
                if k:
                    second(ref, name + "2", u, k).wait_send()
                    third(ref, name + "3", u, k).wait_send()
                fourth(ref, name + "4", u, k).wait_send()
    for k in range(1, 4):
        out_x(k).wait_send()
        back_x(k).wait_send()
    each(1, NZ, lambda k: stat_to(k).wait_send())
    each(1, NZ, lambda k: stat_from(k).wait_send())
    sum_core.wait_send()
    med_core.wait_send()
    each(1, NP, lambda k: sum_plane(k).wait_send())
    for j in range(1, 4):
        sum_far(j).wait_send()
        med_far(j).wait_send()
    for d in range(3):
        sum_near(d).wait_send()
        med_near(d).wait_send()
    each(1, NP, lambda k: all_plane(k).wait_send())
    each(0, NP, lambda p: all_core(p).wait_send())
    each(1, NP, lambda k: med_all(k).wait_send())


def body(frame_features, frame_owner, latents, latent_gain, media_gain, query_proj, keyval_proj, grad_output):
    route = jnp.repeat(frame_owner[0, :, 0], TOK)
    scratch = [pltpu.VMEM(*spec) for spec in BUFFERS.values()]
    scratch += [DMA(shape) for shape in SEMS.values() for _ in range(2)]
    vmem = pl.BlockSpec(memory_space=pltpu.VMEM)
    attended, latent_grad, lat_inverse, latent_gain_grad, media_gain_grad = pl.pallas_call(
        kernel,
        out_shape=(
            jax.ShapeDtypeStruct((LAT, INNER), F32),
            jax.ShapeDtypeStruct((LAT, WIDTH), F32),
            jax.ShapeDtypeStruct((LAT, 128), F32),
            jax.ShapeDtypeStruct((1, WIDTH), F32),
            jax.ShapeDtypeStruct((1, WIDTH), F32),
        ),
        in_specs=[vmem] * len(INPUTS),
        out_specs=(vmem,) * len(OUTPUTS),
        scratch_shapes=scratch,
        compiler_params=pltpu.CompilerParams(collective_id=0, has_side_effects=True, vmem_limit_bytes=60 << 20),
        name="resampler",
    )(
        keyval_proj,
        query_proj,
        frame_features.reshape(ROWS, WIDTH),
        latents,
        latent_gain,
        media_gain,
        jnp.broadcast_to(route[:, None], (ROWS, 128)),
        grad_output[0, 0],
    )
    latent_grad = latent_grad * lat_inverse[:, :1]
    return (attended.astype(BF16)[None, None], latent_grad, latent_gain_grad[0], media_gain_grad[0])


def solution(mesh):
    placed = (
        P("dp", "frame", None, None),
        P("dp", "frame", None),
        P(),
        P(),
        P(),
        P(("dp", "frame"), None),
        P(("dp", "frame"), None),
        P("dp", "frame", None, None),
    )
    return jax.shard_map(
        body,
        mesh=mesh,
        in_specs=placed,
        out_specs=(P("dp", "frame", None, None), P(), P(), P()),
        check_vma=False,
    )
```

```python
import jax
import jax.numpy as jnp
from jax import lax
from jax.experimental import pallas as pl
from jax.experimental.pallas import tpu as pltpu
from jax.sharding import PartitionSpec as P

NX, NY, NZ = 4, 4, 16
NP = NX * NY
HEADS, HEAD, INNER, WIDTH, LAT = 8, 64, 512, 1536, 64
TOK, FRAMES = 8, 32
ROWS = FRAMES * TOK
KEYS = NX * TOK
SLOTS = NZ * TOK
SEND = 2 * INNER + 128
DEAD = -1e30
MESH = pl.DeviceIdType.MESH
F32, BF16 = jnp.float32, jnp.bfloat16
DMA = pltpu.SemaphoreType.DMA


def dot(left, right, dims=((1,), (0,))):
    return lax.dot_general(left, right, (dims, ((), ())), preferred_element_type=F32)


def dot_nt(left, right):
    return dot(left, right, ((1,), (1,)))


def dot_tn(left, right):
    return dot(left, right, ((0,), (0,)))


def norm_rows(values):
    center = values - jnp.mean(values, -1, keepdims=True)
    inverse = lax.rsqrt(jnp.mean(center * center, -1, keepdims=True) + 1e-05)
    return center * inverse, inverse


def iota(shape, dim):
    return lax.broadcasted_iota(jnp.int32, shape, dim)


def gathered_order():
    place = iota((384, 384), 1)
    block = (place >= 96).astype(jnp.int32) + (place >= 192).astype(jnp.int32) + (place >= 288).astype(jnp.int32)
    inner = place - block * 96
    six = (inner * 43) >> 8
    last = inner - six * 6
    odd = (last >= 3).astype(jnp.int32)
    natural = odd * 192 + six * 12 + block * 3 + last - odd * 3
    return jnp.where(iota((384, 384), 0) == natural, 1.0, 0.0).astype(BF16)


def sample_order():
    shape = (NZ * KEYS, NZ * KEYS)
    place = iota(shape, 0)
    source = (((place >> 3) & 3) << 7) + ((place >> 5) << 3) + (place & 7)
    return jnp.where(iota(shape, 1) == source, 1.0, 0.0).astype(BF16)


def source_order():
    shape = (NZ * KEYS, NZ * KEYS)
    place = iota(shape, 0)
    sample = (((place >> 3) & (NZ - 1)) << 5) + ((place >> 7) << 3) + (place & 7)
    return jnp.where(iota(shape, 1) == sample, 1.0, 0.0).astype(BF16)


def by_head(ref, rows):
    for head in range(HEADS):
        lanes = slice(head // 2 * 128, head // 2 * 128 + 128)
        own = (iota((LAT, 128), 1) >> 6) == head % 2
        part = jnp.where(own, rows[:, lanes].astype(F32), 0.0).astype(BF16)
        ref[head * LAT : head * LAT + LAT, lanes] = part


def head_blocks(left, right):
    blocks = []
    for pair in range(HEADS // 2):
        lanes = slice(pair * 128, pair * 128 + 128)
        both = dot_tn(left[:, lanes], right[:, lanes])
        blocks.append(jnp.where(iota((HEAD, 128), 1) < HEAD, both[:HEAD], both[HEAD:]))
    return jnp.concatenate(blocks, axis=1)


def push(src, dst, send, recv, to):
    return pltpu.make_async_remote_copy(
        src_ref=src, dst_ref=dst, send_sem=send, recv_sem=recv, device_id=to, device_id_type=MESH
    )


INPUTS = ("keyval", "query", "frames", "latents", "latent_gain", "media_gain", "route", "grad")
OUTPUTS = ("attended", "latent_grad", "lat_inverse", "latent_gain_grad", "media_gain_grad")
BUFFERS = dict(
    order=((384, 384), BF16),
    sorting=((NZ * KEYS, NZ * KEYS), BF16),
    resorting=((NZ * KEYS, NZ * KEYS), BF16),
    low=((NZ, KEYS, INNER), BF16),
    shard=((2, 8, 768), BF16),
    pair=((2, 8, 768), BF16),
    pair_rows=((8, 768), F32),
    zkv=((NZ, 8, 512), BF16),
    zq=((NZ, 8, 256), BF16),
    rows=((6 * NZ, 768), F32),
    wkv=((2, 2, NY, NX, 6 * NZ, 256), BF16),
    wq=((2, 2, NY, NX, 6 * NZ, 128), BF16),
    gob=((NZ, LAT, INNER), BF16),
    hat=((ROWS, WIDTH), F32),
    normed=((ROWS, WIDTH), BF16),
    kv=((ROWS, SEND), BF16),
    mine=((ROWS, NX * SLOTS), BF16),
    slots=((NX, SLOTS, SEND), BF16),
    got=((NX, SLOTS, SEND), BF16),
    kvs=((NZ, KEYS, SEND), BF16),
    lat_normed=((LAT, WIDTH), BF16),
    lat_hat=((LAT, WIDTH), F32),
    lat_kv=((LAT, 2 * INNER), BF16),
    qrow=((HEADS * LAT, INNER), BF16),
    gorow=((NZ, HEADS * LAT, INNER), BF16),
    scores=((NZ, KEYS, INNER), F32),
    gprob=((NZ, KEYS, INNER), F32),
    lat_scores=((LAT, INNER), F32),
    lat_gprob=((LAT, INNER), F32),
    stat=((NZ, 2, 1, INNER), F32),
    stat_got=((NZ, 2, 1, INNER), F32),
    stat_own=((2, 1, INNER), F32),
    stat_all=((NZ, 2, 1, INNER), F32),
    gs=((NZ, KEYS, INNER), BF16),
    gkv=((NZ, KEYS, 2 * INNER), BF16),
    back=((NX, SLOTS, 2 * INNER), BF16),
    back_got=((NX, SLOTS, 2 * INNER), BF16),
    lat_out=((4, LAT, INNER), F32),
    part=((4, 4, LAT, INNER), BF16),
    near_in=((3, 4, LAT, INNER), BF16),
    far_out=((4, LAT, INNER), BF16),
    far_in=((4, LAT, INNER), BF16),
    own_part=((LAT, INNER), F32),
    sums=((2, NP, 3, 8, 128), F32),
    sums_core=((NP, 3, 8, 128), F32),
    sums_plane=((NP, 3, 8, 128), F32),
    chunk=((3, 8, 128), F32),
    sum_quads=((4, 3, 8, 128), F32),
    sum_class=((4, 3, 8, 128), F32),
    whole=((2, NP, 3, 8, 128), F32),
    media=((12, 1, 128), F32),
    media_core=((12, 1, 128), F32),
    med_quads=((4, 12, 1, 128), F32),
    med_class=((4, 12, 1, 128), F32),
    med_whole=((NP, 12, 1, 128), F32),
)
SEMS = dict(
    swap=(1,), along_z=(NZ,), along_q=(NZ,), go_far=(4,), go_near=(4, 3), kv2=(2, 4), kv3=(2, 4), kv4=(2, 4), q2=(2, 4), q3=(2, 4), q4=(2, 4),
    out_x=(4,), back_x=(4,), stat_to=(NZ,), stat_from=(NZ,), near=(3,), far=(4,), sum_core=(1,), sum_plane=(NP,),
    med_core=(1,), sum_far=(4,), sum_near=(3,), med_far=(4,), med_near=(3,), all_plane=(NP,), all_core=(NP,), med_all=(NP,),
)
NEAR = (1, NZ - 1, 2)


class Refs:
    pass


def kernel(*refs):
    r = Refs()
    names = INPUTS + OUTPUTS + tuple(BUFFERS) + tuple(n + e for n in SEMS for e in ("_s", "_r"))
    for name, ref in zip(names, refs, strict=True):
        setattr(r, name, ref)

    def sems(name, *at):
        return getattr(r, name + "_s").at[at], getattr(r, name + "_r").at[at]

    dp, fr = lax.axis_index("dp"), lax.axis_index("frame")
    y, core, z, x = lax.div(dp, 2), lax.rem(dp, 2), lax.div(fr, NX), lax.rem(fr, NX)
    other, me = 1 - core, y * NX + x

    def device(yy, cc, zz, xx):
        return (yy * 2 + cc, zz * NX + xx)

    partner = device(y, other, z, x)

    def at_z(k):
        zz = lax.rem(z + k, NZ)
        return zz, device(y, core, zz, x)

    def at_x(k):
        xx = lax.rem(x + k, NX)
        return xx, device(y, core, z, xx)

    def at_y(k):
        yy = lax.rem(y + k, NY)
        return yy, device(yy, core, z, x)

    def at_plane(k):
        p = lax.rem(me + k, NP)
        return p, device(lax.div(p, NX), core, z, lax.rem(p, NX))

    def each(lo, hi, act):
        @pl.loop(lo, hi)
        def _(k):
            act(k)

    def far_first(act):
        @pl.loop(0, NZ - 1)
        def _(i):
            act(NZ // 2 + ((i + 1) >> 1) * (1 - 2 * (i & 1)))

    barrier = pltpu.get_barrier_semaphore()

    def greet(to):
        pl.semaphore_signal(barrier, inc=1, device_id=to, device_id_type=MESH)

    far_first(lambda k: greet(at_z(k)[1]))
    each(1, NP, lambda k: greet(at_plane(k)[1]))
    greet(partner)
    r.gob[z] = r.grad[...]
    r.pair_rows[...] = jnp.zeros_like(r.pair_rows)
    for c in range(2):
        r.pair_rows[0:3, 0:512] = r.keyval[:, c * 512 : c * 512 + 512].astype(F32)
        r.pair_rows[0:3, 512:768] = r.query[:, c * 256 : c * 256 + 256].astype(F32)
        r.shard[c] = r.pair_rows[...].astype(BF16)
    r.pair[core] = r.shard[core]
    media_gain = r.media_gain[...].reshape(1, WIDTH)
    latent_gain = r.latent_gain[...].reshape(1, WIDTH)

    @pl.loop(0, ROWS // 32)
    def _(b):
        span = pl.ds(pl.multiple_of(b * 32, 32), 32)
        hat, _ = norm_rows(r.frames[span, :].astype(F32))
        r.hat[span, :] = hat
        r.normed[span, :] = (hat * media_gain).astype(BF16)

    def reorder(ref):
        for i in range(4):
            lanes = slice(i * 384, i * 384 + 384)
            ref[:, lanes] = dot(ref[:, lanes], r.order[...]).astype(BF16)

    r.order[...] = gathered_order()
    r.sorting[...] = sample_order()
    r.resorting[...] = source_order()
    r.qrow[...] = jnp.zeros_like(r.qrow)

    @pl.loop(0, NZ)
    def _(s):
        r.gorow[s] = jnp.zeros((HEADS * LAT, INNER), BF16)

    reorder(r.normed)
    hat, inverse = norm_rows(r.latents[...])
    r.lat_hat[...] = hat
    r.lat_inverse[...] = jnp.broadcast_to(inverse, (LAT, 128))
    r.lat_normed[...] = (hat * latent_gain).astype(BF16)
    reorder(r.lat_normed)
    def slot_owner(slot):
        return ((slot >> 3) & (NZ - 1)) * NX + (slot >> 7)

    slot = iota((ROWS, NX * SLOTS), 1)
    route = jnp.concatenate([r.route[...]] * 4, axis=1)
    mine = (route == slot_owner(slot)) & ((slot & 7) == (iota((ROWS, NX * SLOTS), 0) & 7))
    r.mine[...] = jnp.where(mine, 1.0, 0.0).astype(BF16)
    r.kv[:, 2 * INNER :] = jnp.ones((ROWS, 128), BF16)
    pl.semaphore_wait(barrier, NZ - 1 + NP - 1 + 1)

    swap = push(r.shard.at[other], r.pair.at[core], *sems("swap", 0), partner)
    swap.start()

    def go_far(j):
        return push(r.gob.at[z], r.gob.at[z], *sems("go_far", j), at_z(4 * j)[1])

    def go_near(i, d):
        block = r.gob.at[lax.rem(z + 4 * i, NZ)]
        return push(block, block, *sems("go_near", i, d), at_z(NEAR[d])[1])

    swap.wait()
    r.pair_rows[...] = jnp.zeros_like(r.pair_rows)
    r.pair_rows[0:3] = r.pair[0, 0:3].astype(F32)
    r.pair_rows[3:6] = r.pair[1, 0:3].astype(F32)
    r.zkv[z] = r.pair_rows[:, :512].astype(BF16)
    r.zq[z] = r.pair_rows[:, 512:].astype(BF16)

    def along_z(k):
        return push(r.zkv.at[z], r.zkv.at[z], *sems("along_z", k), at_z(k)[1])

    def along_q(k):
        return push(r.zq.at[z], r.zq.at[z], *sems("along_q", k), at_z(k)[1])

    far_first(lambda k: along_z(k).start())
    far_first(lambda k: along_q(k).start())
    each(1, NZ, lambda k: along_z(k).wait_recv())
    for k in range(NZ):
        r.rows[6 * k : 6 * k + 6, :512] = r.zkv[k, 0:6].astype(F32)
    for u in range(2):
        r.wkv[core, u, y, x] = r.rows[:, u * 256 : u * 256 + 256].astype(BF16)

    def second(ref, name, u, k):
        block = ref.at[core, u, y, x]
        return push(block, block, *sems(name, u, k), (at_y, at_x)[u](k)[1])

    def line(ref, u, turn):
        if u == 0:
            return ref.at[core, 0, :, lax.rem(x + turn, NX)]
        return ref.at[core, 1, lax.rem(y + turn, NY)]

    def third(ref, name, u, k):
        return push(line(ref, u, 0), line(ref, u, 0), *sems(name, u, k), (at_x, at_y)[u](k)[1])

    def fourth(ref, name, u, k):
        return push(line(ref, u, 4 - k), line(ref, u, 4 - k), *sems(name, u, k), partner)

    def for_all(act, *args):
        for k in (1, 3, 2):
            for u in range(2):
                act(*args, u, k)

    for_all(lambda u, k: second(r.wkv, "kv2", u, k).start())
    each(1, NZ, lambda k: along_q(k).wait_recv())
    for k in range(NZ):
        r.rows[6 * k : 6 * k + 6, 512:] = r.zq[k, 0:6].astype(F32)
    for u in range(2):
        r.wq[core, u, y, x] = r.rows[:, 512 + u * 128 : 640 + u * 128].astype(BF16)
    for_all(lambda u, k: second(r.wq, "q2", u, k).start())
    for j in (2, 1, 3):
        go_far(j).start()
    for d in range(3):
        go_near(0, d).start()
    for_all(lambda u, k: second(r.wkv, "kv2", u, k).wait_recv())
    for_all(lambda u, k: third(r.wkv, "kv3", u, k).start())
    for u in range(2):
        fourth(r.wkv, "kv4", u, 0).start()
    for_all(lambda u, k: second(r.wq, "q2", u, k).wait_recv())
    for k in (1, 3, 2):
        for u in range(2):
            third(r.wkv, "kv3", u, k).wait_recv()
            fourth(r.wkv, "kv4", u, k).start()
    for_all(lambda u, k: third(r.wq, "q3", u, k).start())
    for u in range(2):
        fourth(r.wq, "q4", u, 0).start()
    for j in (1, 3, 2):
        go_far(j).wait_recv()
        for d in range(3):
            go_near(4 - j, d).start()
    for k in (0, 1, 3, 2):
        for u in range(2):
            fourth(r.wkv, "kv4", u, k).wait_recv()

    def kv_proj(c, u):
        return r.wkv[c, u].reshape(WIDTH, 256)

    def q_proj(c, u):
        return r.wq[c, u].reshape(WIDTH, 128)

    for c in range(2):
        for u in range(2):
            lanes = slice(c * 512 + u * 256, c * 512 + u * 256 + 256)
            r.kv[:, lanes] = dot(r.normed[...], kv_proj(c, u)).astype(BF16)

    def out_x(k):
        xx, to = at_x(k)
        return push(r.slots.at[xx], r.got.at[x], *sems("out_x", k), to)

    for i in range(NX):
        span = slice(i * SLOTS, i * SLOTS + SLOTS)
        r.slots[i] = dot_tn(r.mine[:, span], r.kv[...]).astype(BF16)
    for k in (1, 3, 2):
        out_x(k).start()
    r.got[x] = r.slots[x]
    for k in (1, 3, 2):
        for u in range(2):
            third(r.wq, "q3", u, k).wait_recv()
            fourth(r.wq, "q4", u, k).start()
    for k in (0, 1, 3, 2):
        for u in range(2):
            fourth(r.wq, "q4", u, k).wait_recv()
    query = jnp.concatenate([dot(r.lat_normed[...], q_proj(c, u)) for c in range(2) for u in range(2)], axis=1)
    by_head(r.qrow, (query * HEAD**-0.5).astype(BF16))
    for c in range(2):
        for u in range(2):
            lanes = slice(c * 512 + u * 256, c * 512 + u * 256 + 256)
            r.lat_kv[:, lanes] = dot(r.lat_normed[...], kv_proj(c, u)).astype(BF16)
    r.lat_scores[...] = dot_nt(r.lat_kv[:, :INNER], r.qrow[...])
    for i in range(4):
        for d in range(3):
            go_near(i, d).wait_recv()

    @pl.loop(0, NZ, unroll=2)
    def _(s):
        by_head(r.gorow.at[s], r.gob[s])

    r.lat_gprob[...] = dot_nt(r.lat_kv[:, INNER:], r.gorow[z])
    for k in (1, 3, 2):
        out_x(k).wait_recv()

    got = r.got[...].reshape(NZ * KEYS, SEND)
    for i in range(4):
        span = slice(i * 128, i * 128 + 128)
        r.kvs[i * 4 : i * 4 + 4] = dot(r.sorting[span], got).astype(BF16).reshape(4, KEYS, SEND)
    r.scores[...] = dot_nt(r.kvs[:, :, :INNER].reshape(NZ * KEYS, INNER), r.qrow[...]).reshape(NZ, KEYS, INNER)

    @pl.loop(0, NZ, unroll=4)
    def _(s):
        live = jnp.concatenate([r.kvs[s, :, 2 * INNER :].astype(F32)] * 4, axis=1)
        scores = jnp.where(live > 0.5, r.scores[s], DEAD)
        gprob = dot_nt(r.kvs[s, :, INNER : 2 * INNER], r.gorow[s])
        top = jnp.max(scores, axis=0, keepdims=True)
        weight = jnp.exp(scores - top)
        r.scores[s] = scores
        r.gprob[s] = gprob
        total = jnp.sum(weight, axis=0, keepdims=True)
        r.stat[s, 0] = top + jnp.log(total)
        r.stat[s, 1] = jnp.sum(weight * gprob, axis=0, keepdims=True) / total

    def stat_to(k):
        zz, to = at_z(k)
        return push(r.stat.at[zz], r.stat_got.at[z], *sems("stat_to", k), to)

    far_first(lambda k: stat_to(k).start())
    r.stat_got[z] = r.stat[z]
    top = jnp.max(r.lat_scores[...], axis=0, keepdims=True)
    weight = jnp.exp(r.lat_scores[...] - top)
    total = jnp.sum(weight, axis=0, keepdims=True)
    mixed = jnp.sum(weight * r.lat_gprob[...], axis=0, keepdims=True)
    each(1, NZ, lambda k: along_z(k).wait_send())
    each(1, NZ, lambda k: along_q(k).wait_send())
    for j in range(1, 4):
        go_far(j).wait_send()
        out_x(j).wait_send()
    for d in range(3):
        for i in range(4):
            go_near(i, d).wait_send()
    for ref, name in ((r.wkv, "kv"), (r.wq, "q")):
        for u in range(2):
            for k in range(4):
                if k:
                    second(ref, name + "2", u, k).wait_send()
                    third(ref, name + "3", u, k).wait_send()
                fourth(ref, name + "4", u, k).wait_send()
    each(1, NZ, lambda k: stat_to(k).wait_recv())
    best = top
    for i in range(NZ):
        best = jnp.maximum(best, r.stat_got[i, 0])
    total = total * jnp.exp(top - best)
    mixed = mixed * jnp.exp(top - best)
    for i in range(NZ):
        factor = jnp.exp(r.stat_got[i, 0] - best)
        total = total + factor
        mixed = mixed + r.stat_got[i, 1] * factor
    r.stat_own[0] = best + jnp.log(total)
    r.stat_own[1] = mixed / total

    def stat_from(k):
        return push(r.stat_own, r.stat_all.at[z], *sems("stat_from", k), at_z(k)[1])

    far_first(lambda k: stat_from(k).start())
    r.stat_all[z] = r.stat_own[...]

    prob = jnp.exp(r.lat_scores[...] - r.stat_own[0])
    lat_low = prob.astype(BF16)
    lat_gs = (prob * (r.lat_gprob[...] - r.stat_own[1])).astype(BF16)
    r.lat_out[0] = head_blocks(lat_gs, r.lat_kv[:, :INNER])
    r.lat_out[1] = dot(lat_gs, r.qrow[...])
    r.lat_out[2] = dot(lat_low, r.gorow[z])
    r.lat_out[3] = head_blocks(lat_low, r.lat_kv[:, INNER:])
    each(1, NZ, lambda k: stat_from(k).wait_recv())

    @pl.loop(0, NZ, unroll=4)
    def _(s):
        prob = jnp.exp(r.scores[s] - r.stat_all[s, 0])
        low = prob.astype(BF16)
        r.gs[s] = (prob * (r.gprob[s] - r.stat_all[s, 1])).astype(BF16)
        r.gkv[s, :, INNER:] = dot(low, r.gorow[s]).astype(BF16)
        r.low[s] = low

    gs = r.gs[...].reshape(NZ * KEYS, INNER)
    r.gkv[:, :, :INNER] = dot(gs, r.qrow[...]).astype(BF16).reshape(NZ, KEYS, INNER)
    gkv = r.gkv[...].reshape(NZ * KEYS, 2 * INNER)

    def back_x(k):
        xx, to = at_x(k)
        return push(r.back.at[xx], r.back_got.at[x], *sems("back_x", k), to)

    for i in range(NX):
        span = slice(i * SLOTS, i * SLOTS + SLOTS)
        r.back[i] = dot(r.resorting[span], gkv).astype(BF16)
    for k in (1, 3, 2):
        back_x(k).start()

    def near(d):
        return push(r.part.at[lax.rem(z + NEAR[d], 4)], r.near_in.at[d], *sems("near", d), at_z(NEAR[d])[1])

    def far(i):
        return push(r.far_out.at[lax.rem(lax.div(z, 4) + i, 4)], r.far_in.at[i], *sems("far", i), at_z(4 * i)[1])

    @pl.loop(0, NZ, unroll=4)
    def _(s):
        r.part[s & 3, s >> 2] = head_blocks(r.low[s], r.kvs[s, :, INNER : 2 * INNER]).astype(BF16)

    for d in range(3):
        near(d).start()
    gquery = (head_blocks(gs, r.kvs[:, :, :INNER].reshape(NZ * KEYS, INNER)) + r.lat_out[0]) * HEAD**-0.5
    own = jnp.concatenate([gquery, r.lat_out[1], r.lat_out[2]], axis=1)
    for c in range(2):
        for p in range(NP):
            for j in range(3):
                first = c * 768 + p % 2 * 384 + j * 128
                r.sums[c, p, j] = own[p // 2 * 8 : p // 2 * 8 + 8, first : first + 128]
    sum_core = push(r.sums.at[other], r.sums_core, *sems("sum_core", 0), partner)
    sum_core.start()
    sum_core.wait_recv()

    @pl.loop(0, NP)
    def _(p):
        r.sums_core[p] = r.sums_core[p] + r.sums[core, p]

    def sum_plane(k):
        p, to = at_plane(k)
        return push(r.sums_core.at[p], r.sums_plane.at[me], *sems("sum_plane", k), to)

    each(1, NP, lambda k: sum_plane(k).start())
    r.sums_plane[me] = r.sums_core[me]
    for k in (1, 3, 2):
        back_x(k).wait_recv()
    r.back_got[x] = r.back[x]

    r.kv[:, : 2 * INNER] = dot(r.mine[...], r.back_got[...].reshape(NX * SLOTS, 2 * INNER)).astype(BF16)
    grad_norm = 0.0
    for c in range(2):
        for u in range(2):
            lanes = slice(c * 512 + u * 256, c * 512 + u * 256 + 256)
            grad_norm = grad_norm + dot_nt(r.kv[:, lanes], kv_proj(c, u))
    r.normed[...] = grad_norm.astype(BF16)
    for i in range(4):
        lanes = slice(i * 384, i * 384 + 384)
        natural = dot_nt(r.normed[:, lanes], r.order[...])
        term = jnp.sum(natural * r.hat[:, lanes], axis=0, keepdims=True)
        for j in range(3):
            r.media[i * 3 + j] = term[:, j * 128 : j * 128 + 128]
    med_core = push(r.media, r.media_core, *sems("med_core", 0), partner)
    med_core.start()
    each(1, NP, lambda k: sum_plane(k).wait_recv())
    partial = r.sums_plane[0]
    for p in range(1, NP):
        partial = partial + r.sums_plane[p]
    r.chunk[...] = partial

    def z_far(src, got, name, j):
        return push(src, got.at[lax.div(z, 4)], *sems(name, j), at_z(4 * j)[1])

    def z_near(got, name, d):
        block = got.at[lax.rem(z, 4)]
        return push(block, block, *sems(name, d), at_z(NEAR[d])[1])

    def four(ref):
        return ref[0] + ref[1] + ref[2] + ref[3]

    def sum_far(j):
        return z_far(r.chunk, r.sum_quads, "sum_far", j)

    def sum_near(d):
        return z_near(r.sum_class, "sum_near", d)

    def med_far(j):
        return z_far(r.media_core, r.med_quads, "med_far", j)

    def med_near(d):
        return z_near(r.med_class, "med_near", d)

    for j in (2, 1, 3):
        sum_far(j).start()
    r.sum_quads[lax.div(z, 4)] = r.chunk[...]
    med_core.wait_recv()

    r.media_core[...] = r.media_core[...] + r.media[...]

    for j in (2, 1, 3):
        med_far(j).start()
    r.med_quads[lax.div(z, 4)] = r.media_core[...]
    for d in range(3):
        near(d).wait_recv()
    for j in range(4):
        value = r.part[lax.rem(z, 4), j].astype(F32)
        for d in range(3):
            value = value + r.near_in[d, j].astype(F32)
        r.far_out[j] = value.astype(BF16)

        @pl.when(lax.div(z, 4) == j)
        def _():
            r.own_part[...] = value

    for i in range(1, 4):
        far(i).start()
    for j in range(1, 4):
        sum_far(j).wait_recv()
    r.sum_class[lax.rem(z, 4)] = four(r.sum_quads)
    for d in range(3):
        sum_near(d).start()
    def all_plane(k):
        block = r.whole.at[core, me]
        return push(block, block, *sems("all_plane", k), at_plane(k)[1])

    def all_core(p):
        block = r.whole.at[core, p]
        return push(block, block, *sems("all_core", p), partner)

    def med_all(k):
        block = r.med_whole.at[me]
        return push(block, block, *sems("med_all", k), at_plane(k)[1])

    for j in range(1, 4):
        med_far(j).wait_recv()
    r.med_class[lax.rem(z, 4)] = four(r.med_quads)
    for d in range(3):
        med_near(d).start()
    for d in range(3):
        sum_near(d).wait_recv()
    r.whole[core, me] = four(r.sum_class)
    each(1, NP, lambda k: all_plane(k).start())
    all_core(me).start()
    for d in range(3):
        med_near(d).wait_recv()
    r.med_whole[me] = four(r.med_class)
    each(1, NP, lambda k: med_all(k).start())

    each(1, NZ, lambda k: stat_to(k).wait_send())
    for k in range(1, 4):
        back_x(k).wait_send()
    for d in range(3):
        near(d).wait_send()
    sum_core.wait_send()
    med_core.wait_send()
    each(1, NP, lambda k: sum_plane(k).wait_send())

    def forward(k):
        all_plane(k).wait_recv()
        all_core(lax.rem(me + NP - k, NP)).start()

    each(1, NP, forward)
    each(0, NP, lambda p: all_core(p).wait_recv())

    def gathered(c, rows, g, j):
        return r.whole[c, rows * 2 + g, j]

    strips = []
    for c in range(2):
        for g in range(2):
            for j in range(3):
                strips.append(jnp.concatenate([gathered(c, rows, g, j) for rows in range(8)], axis=0))

    def precise(values, weight):
        high = values.astype(BF16)
        low = (values - high.astype(F32)).astype(BF16)
        result = dot_nt(jnp.concatenate([high, low], axis=0), weight)
        return result[:LAT] + result[LAT:]

    grad = 0.0
    for i in range(4):
        grad = grad + precise(strips[i], q_proj(i // 2, i % 2))
        both = jnp.concatenate([strips[4 + 2 * i], strips[5 + 2 * i]], axis=1)
        grad = grad + precise(both, kv_proj(i // 2, i % 2))
    natural = []
    for i in range(4):
        rest = grad[:, i * 384 : i * 384 + 384]
        pieces = []
        for _ in range(3):
            high = rest.astype(BF16)
            rest = rest - high.astype(F32)
            pieces.append(high)
        moved = dot_nt(jnp.concatenate(pieces, axis=0), r.order[...])
        natural.append(moved[:LAT] + moved[LAT : 2 * LAT] + moved[2 * LAT :])
    grad = jnp.concatenate(natural, axis=1)
    hat = r.lat_hat[...]
    r.latent_gain_grad[...] = jnp.sum(grad * hat, axis=0, keepdims=True)
    grad_hat = grad * latent_gain
    r.latent_grad[...] = (
        grad_hat
        - jnp.mean(grad_hat, -1, keepdims=True)
        - hat * jnp.mean(grad_hat * hat, -1, keepdims=True)
    )
    value = r.own_part[...] + r.lat_out[3]
    for i in range(1, 4):
        far(i).wait_recv()
        value = value + r.far_in[i].astype(F32)
    r.attended[...] = value
    each(1, NP, lambda k: med_all(k).wait_recv())
    value = r.med_whole[0]
    for p in range(1, NP):
        value = value + r.med_whole[p]
    for i in range(12):
        r.media_gain_grad[:, i * 128 : i * 128 + 128] = value[i]
    each(1, NZ, lambda k: stat_from(k).wait_send())
    for j in range(1, 4):
        far(j).wait_send()
        sum_far(j).wait_send()
        med_far(j).wait_send()
    for d in range(3):
        sum_near(d).wait_send()
        med_near(d).wait_send()
    each(1, NP, lambda k: all_plane(k).wait_send())
    each(0, NP, lambda p: all_core(p).wait_send())
    each(1, NP, lambda k: med_all(k).wait_send())


def body(frame_features, frame_owner, latents, latent_gain, media_gain, query_proj, keyval_proj, grad_output):
    route = jnp.repeat(frame_owner[0, :, 0], TOK)
    scratch = [pltpu.VMEM(*spec) for spec in BUFFERS.values()]
    scratch += [DMA(shape) for shape in SEMS.values() for _ in range(2)]
    vmem = pl.BlockSpec(memory_space=pltpu.VMEM)
    attended, latent_grad, lat_inverse, latent_gain_grad, media_gain_grad = pl.pallas_call(
        kernel,
        out_shape=(
            jax.ShapeDtypeStruct((LAT, INNER), F32),
            jax.ShapeDtypeStruct((LAT, WIDTH), F32),
            jax.ShapeDtypeStruct((LAT, 128), F32),
            jax.ShapeDtypeStruct((1, WIDTH), F32),
            jax.ShapeDtypeStruct((1, WIDTH), F32),
        ),
        in_specs=[vmem] * len(INPUTS),
        out_specs=(vmem,) * len(OUTPUTS),
        scratch_shapes=scratch,
        compiler_params=pltpu.CompilerParams(collective_id=0, has_side_effects=True, vmem_limit_bytes=60 << 20),
        name="resampler",
    )(
        keyval_proj,
        query_proj,
        frame_features.reshape(ROWS, WIDTH),
        latents,
        latent_gain,
        media_gain,
        jnp.broadcast_to(route[:, None], (ROWS, 128)),
        grad_output[0, 0],
    )
    latent_grad = latent_grad * lat_inverse[:, :1]
    return (attended.astype(BF16)[None, None], latent_grad, latent_gain_grad[0], media_gain_grad[0])


def solution(mesh):
    placed = (
        P("dp", "frame", None, None),
        P("dp", "frame", None),
        P(),
        P(),
        P(),
        P(("dp", "frame"), None),
        P(("dp", "frame"), None),
        P("dp", "frame", None, None),
    )
    return jax.shard_map(
        body,
        mesh=mesh,
        in_specs=placed,
        out_specs=(P("dp", "frame", None, None), P(), P(), P()),
        check_vma=False,
    )
```
